512 devices in a mesh: pairs: 64 (over z, x), seg: 8 (over y, core).
Axes of the slice: x: 4, y: 4, z: 16, core: 2. Of those that a mesh axis runs over, the one named last changes fastest.
Arguments:
- waveform: bfloat16 [2048, 8, 7680], P('pairs', 'seg'), may hold values from -6 to 6
- requests: int32 [64, 256], replicated, may hold values from 0 to 2047, as said below
- pair_list: int32 [64, 256, 2], P('pairs'), may hold values from 0 to 255, as said below
- pair_count: int32 [64], P('pairs'), may hold values from 64 to 256, as said below
Outputs:
- stacks: float32 [16384, 5120], P(('pairs', 'seg'))
The draws below stay inside these ranges and needn't reach their ends.
Inputs may be any that keep to these rules, and one draw needn't show every extreme that they name: `requests`: each row lists 256 different stations in increasing order; station s belongs to owner s // 32; no owner has more than 8 stations in a row, and in every row some owner has exactly 8. `pair_list`: positions in the tile's request list; the two positions of a pair differ. `pair_count`: some tile has all 256 slots live.
All inputs are finite; a program needn't handle non-finite values.
Results may differ from the reference program's by a relative error of at most 0.0064.
Values may be sent and summed in bfloat16 or wider, within the bound.
A program may use at most 64 MiB of HBM per device.

```python
import math
import jax
import jax.numpy as jnp
from jax import lax

STA_DEV = 32
P_TILE = 256
CAP = 8
SAMPLES = 7680
K0 = 16
FB = 1024
HALF_WIN = 64
MAXLAG = 2560
LAGS = 5120
STATIONS = 2048
SEGS = 8
REQ = 256
N_PAIRS = 64


def draw_requests(key, part):

    def one_tile(tile_key):
        key_perm, key_prio, key_full = jax.random.split(tile_key, 3)
        locals_all = jax.vmap(lambda sub: jax.random.permutation(sub, STA_DEV))(jax.random.split(key_perm, N_PAIRS))
        owners = jnp.arange(N_PAIRS, dtype=jnp.int32)
        candidates = (owners[:, None] * STA_DEV + locals_all[:, :CAP]).reshape(-1)
        priority = jax.random.permutation(key_prio, N_PAIRS * CAP)
        full_owner = jax.random.randint(key_full, (), 0, N_PAIRS)
        owner_of = jnp.arange(N_PAIRS * CAP, dtype=jnp.int32) // CAP
        priority = priority + jnp.where(owner_of == full_owner, N_PAIRS * CAP, 0)
        order = jnp.argsort(-priority)
        return jnp.sort(candidates[order[:REQ]])
    return jax.vmap(one_tile)(jax.random.split(jax.random.fold_in(key, 11), N_PAIRS)).astype(jnp.int32)


def draw_pair_list(key, part):
    key_first, key_step = jax.random.split(jax.random.fold_in(key, 23))
    first = jax.random.randint(key_first, (N_PAIRS, P_TILE), 0, REQ)
    step = jax.random.randint(key_step, (N_PAIRS, P_TILE), 1, REQ)
    second = (first + step) % REQ
    return jnp.stack([first, second], axis=-1).astype(jnp.int32)


def draw_pair_count(key, part):
    key_count, key_full = jax.random.split(jax.random.fold_in(key, 37))
    counts = jax.random.randint(key_count, (N_PAIRS,), P_TILE // 4, P_TILE + 1)
    full_tile = jax.random.randint(key_full, (), 0, N_PAIRS)
    return jnp.where(jnp.arange(N_PAIRS) == full_tile, P_TILE, counts).astype(jnp.int32)


def shard_levels(key, extent, shards, smallest, high):
    factor_of = 1.0
    for axis_at, blocks in shards:
        heights = jax.random.uniform(jax.random.fold_in(jax.random.fold_in(key, 6), axis_at), (blocks,), jnp.float32, smallest / len(shards), high / len(shards))
        factor_of = factor_of * jnp.repeat(jnp.exp(heights), extent[axis_at] // blocks).reshape((-1,) + (1,) * (len(extent) - 1 - axis_at))
    return factor_of


def normal_values(own_key, shape, spread, bound, cuts=(), held_as=jnp.bfloat16):
    values = jax.random.normal(own_key, shape, jnp.float32) * spread
    if len(cuts) > 0:
        values = shard_levels(own_key, shape, cuts, -0.22, 0.18) * values
    return jnp.clip(values, min=-bound, max=bound).astype(held_as)


def setup_inputs(seed: int = 0) -> dict:
    seeds = jax.random.split(jax.random.key(seed), 5)
    return {
        "waveform": normal_values(seeds[0], (STATIONS, SEGS, SAMPLES), 1.0, 6.0, ((0, 64), (1, 8))),
        "requests": draw_requests(jax.random.fold_in(seeds[4], 71), 0),
        "pair_list": draw_pair_list(jax.random.fold_in(seeds[4], 71), 0),
        "pair_count": draw_pair_count(jax.random.fold_in(seeds[4], 71), 0),
    }


def band_table(times):
    bins = K0 + jnp.arange(FB, dtype=jnp.int32)
    phase = jnp.mod(times[:, None] * bins[None, :], SAMPLES)
    angle = phase.astype(jnp.float32) * (2.0 * math.pi / SAMPLES)
    return jnp.concatenate([jnp.cos(angle), -jnp.sin(angle)], axis=1).astype(jnp.bfloat16)

def smoother():
    index = jnp.arange(FB, dtype=jnp.int32)
    near = (jnp.abs(index[:, None] - index[None, :]) <= HALF_WIN).astype(jnp.float32)
    return near / lax.optimization_barrier(jnp.sum(near, axis=0, keepdims=True))

def whiten(spectrum):
    real_part = spectrum[:, :FB]
    imag_part = spectrum[:, FB:]
    power = real_part * real_part + imag_part * imag_part
    smooth = jnp.dot(power, smoother(), precision=lax.Precision.HIGHEST)
    scale = 1.0 / jnp.sqrt(smooth + 1e-06)
    return jnp.concatenate([real_part * scale, imag_part * scale], axis=1).astype(jnp.bfloat16)

def cross(first, second):
    first = first.astype(jnp.float32)
    second = second.astype(jnp.float32)
    first_re, first_im = (first[..., :FB], first[..., FB:])
    second_re, second_im = (second[..., :FB], second[..., FB:])
    real_part = first_re * second_re + first_im * second_im
    imag_part = first_im * second_re - first_re * second_im
    return jnp.concatenate([real_part, imag_part], axis=-1)

def reference(waveform, requests, pair_list, pair_count):
    signal = waveform.reshape(STATIONS * SEGS, SAMPLES)
    spectrum = jnp.dot(signal, band_table(jnp.arange(SAMPLES, dtype=jnp.int32)), preferred_element_type=jnp.float32)
    whitened = whiten(spectrum).reshape(STATIONS, SEGS, 2 * FB)

    def one_tile(operands):
        wanted, listed, live_count = operands
        first = whitened[wanted[listed[:, 0]]]
        second = whitened[wanted[listed[:, 1]]]
        summed = lax.optimization_barrier(jnp.sum(cross(first, second), axis=1))
        live = (jnp.arange(P_TILE, dtype=jnp.int32) < live_count)[:, None]
        return jnp.where(live, summed, 0.0).astype(jnp.bfloat16)
    stacked = lax.map(one_tile, (requests, pair_list, pair_count)).reshape(P_TILE * N_PAIRS, 2 * FB)
    shifts = jnp.arange(LAGS, dtype=jnp.int32) - MAXLAG
    lagged = lax.dot_general(stacked, band_table(shifts), (((1,), (1,)), ((), ())), preferred_element_type=jnp.float32)
    return lagged * (1.0 / math.sqrt(FB * SEGS))
```

```python
import functools
import math

import jax
import jax.numpy as jnp
import ml_dtypes
import numpy as np
from jax import lax
from jax.experimental import pallas as pl
from jax.experimental.pallas import tpu as pltpu
from jax.sharding import PartitionSpec as P

SAMPLES = 7680
K0 = 16
FB = 1024
HALF_WIN = 64
MAXLAG = 2560
LAGS = 5120
QUARTER = SAMPLES // 4
SUB = FB // 4
NZ, NX, NY, NC = 16, 4, 4, 2
STA = 32
TILE = 256
CHUNK = 640
DEAD = 4095
VMEM_BYTES = 56 * 1024 * 1024
F32 = jnp.float32
BF16 = jnp.bfloat16
I32 = jnp.int32


def wave_tables():
    bins = np.concatenate([K0 + 4 * np.arange(SUB) + r for r in range(4)])
    phase = (np.arange(QUARTER)[:, None] * bins[None, :]) % SAMPLES
    angle = phase.astype(np.float32) * np.float32(2.0 * math.pi / SAMPLES)
    cos = np.cos(angle).astype(ml_dtypes.bfloat16)
    sin = np.sin(angle).astype(ml_dtypes.bfloat16)
    forward = np.stack([np.concatenate([cos[:, SUB * r : SUB * (r + 1)], sin[:, SUB * r : SUB * (r + 1)]], axis=1) for r in range(4)])
    lag = np.stack(
        [
            np.concatenate([cos[CHUNK * i : CHUNK * (i + 1)].T, sin[CHUNK * i : CHUNK * (i + 1)].T], axis=1)
            for i in range(QUARTER // CHUNK)
        ]
    )
    return forward, lag


def iota(shape, dim):
    return lax.broadcasted_iota(I32, shape, dim)


def where_am_i():
    tile = lax.axis_index("pairs")
    seg = lax.axis_index("seg")
    return tile // NX, tile % NX, seg // NC, seg % NC


def at(z, x, y, c):
    return (z * NX + x, y * NC + c)


def row_of_station(station):
    owner = lax.shift_right_logical(station, 5)
    return (owner & 3) * (NZ * STA) + lax.shift_right_logical(owner, 2) * STA + (station & 31)


def spectra_kernel(count_ref, wave_ref, table_ref, requests_ref, pairs_ref, out_ref, index_ref, spec_ref):
    residue = pl.program_id(0)

    def quarter(i):
        return wave_ref[:, QUARTER * i : QUARTER * (i + 1)].astype(F32)

    def times_table(lhs):
        return jnp.dot(lhs.astype(BF16), table_ref[0], preferred_element_type=F32)

    @pl.when(residue == 0)
    def _():
        out = times_table((quarter(0) + quarter(2)) + (quarter(1) + quarter(3)))
        spec_ref[0, :STA] = out[:, :SUB]
        spec_ref[0, STA:] = -out[:, SUB:]
        tile = lax.axis_index("pairs")
        wanted = requests_ref[pl.ds(tile, 1), :].astype(F32)
        eye = iota((TILE, TILE), 0) == iota((TILE, TILE), 1)
        wanted_col = jnp.sum(jnp.where(eye, wanted, 0.0), axis=1, keepdims=True)
        ends = []
        for end in range(2):
            hit = iota((TILE, TILE), 0) == pairs_ref[end : end + 1, :]
            station = jnp.sum(jnp.where(hit, wanted_col, 0.0), axis=0, keepdims=True).astype(I32)
            ends.append(row_of_station(station))
        live = iota((1, TILE), 1) < count_ref[0]
        index_ref[0] = jnp.where(live, ends[0] * 4096 + ends[1], DEAD * 4096 + DEAD)

    @pl.when(residue == 2)
    def _():
        out = times_table((quarter(0) + quarter(2)) - (quarter(1) + quarter(3)))
        spec_ref[2, :STA] = out[:, :SUB]
        spec_ref[2, STA:] = -out[:, SUB:]

    def odd(sign):
        out = times_table(jnp.concatenate([quarter(0) - quarter(2), quarter(1) - quarter(3)], axis=0))
        a_cos, a_sin = out[:STA, :SUB], out[:STA, SUB:]
        b_cos, b_sin = out[STA:, :SUB], out[STA:, SUB:]
        return a_cos + sign * b_sin, sign * b_cos - a_sin

    @pl.when(residue == 1)
    def _():
        re, im = odd(-1.0)
        spec_ref[1, :STA] = re
        spec_ref[1, STA:] = im

    @pl.when(residue == 3)
    def _():
        re, im = odd(1.0)
        spec_ref[3, :STA] = re
        spec_ref[3, STA:] = im
        power = []
        for r in range(4):
            one, two = spec_ref[r, :STA], spec_ref[r, STA:]
            power.append(one * one + two * two)
        power = jnp.concatenate(power, axis=0)
        high = power.astype(BF16)
        low = (power - high.astype(F32)).astype(BF16)
        parts = jnp.concatenate([high, low], axis=0)
        apart = iota((SUB, SUB), 0) - iota((SUB, SUB), 1)

        def band(lowest, highest):
            near = jnp.where((apart >= lowest) & (apart <= highest), 1.0, 0.0).astype(BF16)
            both = jnp.dot(parts, near, preferred_element_type=F32)
            return both[: 4 * STA] + both[4 * STA :]

        same = band(-16, 16)
        after = band(-15, 16)
        before = band(-16, 15)
        lane = iota((STA, 128), 1)
        for r in range(4):
            total = same[STA * r : STA * (r + 1)]
            for other in range(4):
                if other < r:
                    total = total + after[STA * other : STA * (other + 1)]
                elif other > r:
                    total = total + before[STA * other : STA * (other + 1)]
            j = 4 * iota((STA, SUB), 1) + r
            count = jnp.minimum(j + HALF_WIN, FB - 1) - jnp.maximum(j - HALF_WIN, 0) + 1
            scale = lax.rsqrt(total / count.astype(F32) + 1e-6)
            re = spec_ref[r, :STA] * scale
            im = spec_ref[r, STA:] * scale
            for g in range(2):
                re_g, im_g = re[:, 128 * g : 128 * (g + 1)], im[:, 128 * g : 128 * (g + 1)]
                block = 4 * r + 2 * g
                out_ref[block] = jnp.where(lane < 64, re_g, pltpu.roll(im_g, 64, 1)).astype(BF16)
                out_ref[block + 1] = jnp.where(lane < 64, pltpu.roll(re_g, 64, 1), im_g).astype(BF16)


def spectra(wave, requests, pairs, count, table):
    return pl.pallas_call(
        spectra_kernel,
        grid=(4,),
        out_shape=(
            jax.ShapeDtypeStruct((NZ, STA, 128), BF16),
            jax.ShapeDtypeStruct((1, 1, TILE), I32),
        ),
        in_specs=[
            pl.BlockSpec(memory_space=pltpu.SMEM),
            pl.BlockSpec((STA, SAMPLES), lambda r: (0, 0)),
            pl.BlockSpec((1, QUARTER, 2 * SUB), lambda r: (r, 0, 0)),
            pl.BlockSpec(requests.shape, lambda r: (0, 0)),
            pl.BlockSpec((2, TILE), lambda r: (0, 0)),
        ],
        out_specs=(
            pl.BlockSpec((NZ, STA, 128), lambda r: (0, 0, 0)),
            pl.BlockSpec((1, 1, TILE), lambda r: (0, 0, 0)),
        ),
        scratch_shapes=[pltpu.VMEM((4, 2 * STA, SUB), F32)],
        compiler_params=pltpu.CompilerParams(vmem_limit_bytes=VMEM_BYTES),
        name="spectra",
    )(count, wave, table, requests, pairs)


def greet(peers):
    barrier = pltpu.get_barrier_semaphore()
    for peer in peers:
        pl.semaphore_signal(barrier, inc=1, device_id=peer, device_id_type=pl.DeviceIdType.MESH)
    pl.semaphore_wait(barrier, len(peers))


def remote(src, dst, send, recv, peer):
    return pltpu.make_async_remote_copy(
        src_ref=src, dst_ref=dst, send_sem=send, recv_sem=recv, device_id=peer, device_id_type=pl.DeviceIdType.MESH
    )


def share_kernel(
    block_ref, index_ref, all_ref, indices_ref, z_send, z_recv, i_send, i_recv, xy_send, xy_recv, own_sem
):
    z, x, y, c = where_am_i()
    z_peer = [at((z + d) % NZ, x, y, c) for d in range(1, NZ)]
    x_peer = [at(z, (x + d) % NX, y, c) for d in range(1, NX)]
    y_peer = [at(z, x, (y + d) % NY, c) for d in range(1, NY)]
    greet(z_peer + x_peer + y_peer)

    def part(half, xs, ys):
        rows = pl.ds(pl.multiple_of(xs * (NZ * STA) + half * (NZ * STA // 2), 256), NZ * STA // 2)
        return all_ref.at[rows, pl.ds(pl.multiple_of(ys * 128, 128), 128)]

    def rows_of(zs):
        rows = pl.ds(pl.multiple_of(x * (NZ * STA) + zs * STA, STA), STA)
        return all_ref.at[rows, pl.ds(pl.multiple_of(y * 128, 128), 128)]

    sent = []
    for d in (8, 7, 9, 6, 10, 5, 11, 4, 12, 3, 13, 2, 14, 1, 15):
        to = (z + d) % NZ
        copy = remote(block_ref.at[to], rows_of(z), z_send.at[d], z_recv.at[z], z_peer[d - 1])
        copy.start()
        sent.append(copy)
    own = pltpu.make_async_copy(block_ref.at[z], rows_of(z), own_sem.at[0])
    own.start()
    own_index = pltpu.make_async_copy(index_ref.at[0], indices_ref.at[z], own_sem.at[1])
    own_index.start()
    for d in range(1, NZ):
        copy = remote(index_ref.at[0], indices_ref.at[z], i_send.at[d], i_recv.at[z], z_peer[d - 1])
        copy.start()
        sent.append(copy)
    own.wait()
    own_index.wait()

    def arrived(half):
        for k in range(NZ // 2):
            zs = half * (NZ // 2) + k

            @pl.when(zs != z)
            def _():
                remote(block_ref.at[0], rows_of(zs), z_send.at[0], z_recv.at[zs], z_peer[0]).wait_recv()

    counter = [0]

    def give(half, xs, ys, peers):
        for peer in peers:
            ref = part(half, xs, ys)
            copy = remote(ref, ref, xy_send.at[counter[0]], xy_recv.at[half, xs, ys], peer)
            counter[0] += 1
            copy.start()
            sent.append(copy)

    def take(half, xs, ys):
        ref = part(half, xs, ys)
        remote(ref, ref, xy_send.at[0], xy_recv.at[half, xs, ys], z_peer[0]).wait_recv()

    arrived(0)
    give(0, x, y, x_peer + y_peer)
    arrived(1)
    give(1, x, y, y_peer + x_peer)
    for d in (1, 3, 2):
        xs, ys = (x + d) % NX, (y + d) % NY
        take(0, xs, y)
        give(0, xs, y, y_peer)
        take(1, x, ys)
        give(1, x, ys, x_peer)
    for d in range(1, NX):
        xs, ys = (x + d) % NX, (y + d) % NY
        take(0, x, ys)
        take(1, xs, y)
        for e in range(1, NY):
            take(0, xs, (y + e) % NY)
            take(1, (x + e) % NX, ys)
    for d in range(1, NZ):
        zs = (z + d) % NZ
        remote(index_ref.at[0], indices_ref.at[zs], i_send.at[0], i_recv.at[zs], z_peer[0]).wait_recv()
    for copy in sent:
        copy.wait_send()


def share(blocks, index):
    dma = pltpu.SemaphoreType.DMA
    return pl.pallas_call(
        share_kernel,
        out_shape=(
            jax.ShapeDtypeStruct((NX * NZ * STA, NY * 128), BF16),
            jax.ShapeDtypeStruct((NZ, 1, TILE), I32),
        ),
        in_specs=[pl.BlockSpec(memory_space=pl.ANY)] * 2,
        out_specs=(pl.BlockSpec(memory_space=pl.ANY),) * 2,
        scratch_shapes=[
            dma((NZ,)),
            dma((NZ,)),
            dma((NZ,)),
            dma((NZ,)),
            dma((2 * (NX * NY - 1),)),
            dma((2, NX, NY)),
            dma((2,)),
        ],
        compiler_params=pltpu.CompilerParams(collective_id=0, has_side_effects=True, vmem_limit_bytes=VMEM_BYTES),
        name="share",
    )(blocks, index)


def cross_kernel(all_ref, indices_ref, out_ref):
    y = lax.axis_index("seg") // NC
    slots = 2 * STA
    pick = iota((slots, TILE), 1) == iota((slots, TILE), 0) + slots * y
    firsts, seconds = [], []
    for k in range(4):
        packed = indices_ref[k]
        first = lax.shift_right_logical(packed, 12).astype(F32)
        second = (packed & 4095).astype(F32)
        firsts.append(jnp.sum(jnp.where(pick, first, 0.0), axis=1, keepdims=True))
        seconds.append(jnp.sum(jnp.where(pick, second, 0.0), axis=1, keepdims=True))
    rows = jnp.concatenate(firsts + seconds, axis=0).astype(I32)
    size = NX * NZ * STA
    hot = jnp.where(iota((8 * slots, size), 1) == rows, 1.0, 0.0).astype(BF16)
    both = jnp.dot(hot, all_ref[...], preferred_element_type=F32)
    straight, turned = 0.0, 0.0
    for s in range(NY):
        first = both[: 4 * slots, 128 * s : 128 * (s + 1)]
        second = both[4 * slots :, 128 * s : 128 * (s + 1)]
        straight = straight + first * second
        turned = turned + first * pltpu.roll(second, 64, 1)
    lane = iota((4 * slots, 128), 1)
    value = jnp.where(lane < 64, straight + pltpu.roll(straight, 64, 1), turned - pltpu.roll(turned, 64, 1))
    for k in range(4):
        for core in range(NC):
            out_ref[core, k] = value[slots * k + STA * core : slots * k + STA * (core + 1)]


def crosses(spectra_all, indices):
    return pl.pallas_call(
        cross_kernel,
        grid=(4,),
        out_shape=jax.ShapeDtypeStruct((NC, NZ, STA, 128), F32),
        in_specs=[
            pl.BlockSpec((NX * NZ * STA, NY * 128), lambda g: (0, 0)),
            pl.BlockSpec((4, 1, TILE), lambda g: (g, 0, 0)),
        ],
        out_specs=pl.BlockSpec((NC, 4, STA, 128), lambda g: (0, g, 0, 0)),
        compiler_params=pltpu.CompilerParams(vmem_limit_bytes=VMEM_BYTES),
        name="crosses",
    )(spectra_all, indices)


def collect_kernel(part_ref, out_ref, other, stack, c_send, c_recv, z_send, z_recv, own_sem):
    z, x, y, c = where_am_i()
    z_peer = [at((z + d) % NZ, x, y, c) for d in range(1, NZ)]
    partner = at(z, x, y, 1 - c)
    greet(z_peer + [partner])
    swap = remote(part_ref.at[1 - c], other, c_send.at[0], c_recv.at[0], partner)
    swap.start()
    swap.wait_recv()
    for k in range(NZ):
        stack[k] = (part_ref[c, k] + other[k]).astype(BF16)
    sent = [swap]
    for d in (8, 7, 9, 6, 10, 5, 11, 4, 12, 3, 13, 2, 14, 1, 15):
        copy = remote(stack.at[(z + d) % NZ], out_ref.at[z], z_send.at[d], z_recv.at[z], z_peer[d - 1])
        copy.start()
        sent.append(copy)
    own = pltpu.make_async_copy(stack.at[z], out_ref.at[z], own_sem.at[0])
    own.start()
    own.wait()
    for d in range(1, NZ):
        zs = (z + d) % NZ
        remote(stack.at[0], out_ref.at[zs], z_send.at[0], z_recv.at[zs], z_peer[0]).wait_recv()
    for copy in sent:
        copy.wait_send()


def collect(parts):
    dma = pltpu.SemaphoreType.DMA
    return pl.pallas_call(
        collect_kernel,
        out_shape=jax.ShapeDtypeStruct((NZ, STA, 128), BF16),
        in_specs=[pl.BlockSpec(memory_space=pltpu.VMEM)],
        out_specs=pl.BlockSpec(memory_space=pl.ANY),
        scratch_shapes=[
            pltpu.VMEM((NZ, STA, 128), F32),
            pltpu.VMEM((NZ, STA, 128), BF16),
            dma((1,)),
            dma((1,)),
            dma((NZ,)),
            dma((NZ,)),
            dma((1,)),
        ],
        compiler_params=pltpu.CompilerParams(collective_id=1, has_side_effects=True, vmem_limit_bytes=VMEM_BYTES),
        name="collect",
    )(parts)


def lag_chunk(stack, table, out_ref, chunk):
    lane = iota((STA, 128), 1)
    sides = []
    for r in range(4):
        re, im = [], []
        for g in range(2):
            one = stack[4 * r + 2 * g].astype(F32)
            two = stack[4 * r + 2 * g + 1].astype(F32)
            re.append(jnp.where(lane < 64, one, pltpu.roll(two, 64, 1)))
            im.append(jnp.where(lane < 64, pltpu.roll(one, 64, 1), two))
        sides.append((jnp.concatenate(re, axis=1).astype(BF16), jnp.concatenate(im, axis=1).astype(BF16)))

    def dot(lhs, r, sine):
        rows = slice(SUB * r, SUB * (r + 1))
        return jnp.dot(lhs, table[rows, CHUNK * sine : CHUNK * (sine + 1)], preferred_element_type=F32)

    even, odd = [], []
    for r in (0, 2):
        even.append(dot(sides[r][0], r, 0) - dot(sides[r][1], r, 1))
    for r in (1, 3):
        lhs = jnp.concatenate(sides[r], axis=0)
        cos, sin = dot(lhs, r, 0), dot(lhs, r, 1)
        odd.append((cos[:STA] - sin[STA:], sin[:STA] + cos[STA:]))
    scale = 1.0 / math.sqrt(FB * NY * NC)
    plus, minus = (even[0] + even[1]) * scale, (even[0] - even[1]) * scale
    real = (odd[0][0] + odd[1][0]) * scale
    imag = (odd[0][1] - odd[1][1]) * scale

    def put(turns, value):
        lag = MAXLAG + QUARTER * turns + CHUNK * chunk
        if 0 <= lag < LAGS:
            out_ref[:, lag : lag + CHUNK] = value

    put(0, plus + real)
    put(-2, plus - real)
    put(1, minus - imag)
    put(-1, minus + imag)


def lags_kernel(stack_ref, table_ref, out_ref):
    for chunk in range(QUARTER // CHUNK):

        @pl.when(pl.program_id(0) == chunk)
        def _():
            lag_chunk([stack_ref[k] for k in range(NZ)], table_ref.at[0], out_ref, chunk)


def lags(stacked, table):
    return pl.pallas_call(
        lags_kernel,
        grid=(QUARTER // CHUNK,),
        out_shape=jax.ShapeDtypeStruct((STA, LAGS), F32),
        in_specs=[
            pl.BlockSpec((NZ, STA, 128), lambda i: (0, 0, 0)),
            pl.BlockSpec((1, FB, 2 * CHUNK), lambda i: (i, 0, 0)),
        ],
        out_specs=pl.BlockSpec((STA, LAGS), lambda i: (0, 0)),
        compiler_params=pltpu.CompilerParams(vmem_limit_bytes=VMEM_BYTES),
        name="lags",
    )(stacked, table)


def body(forward, lag, waveform, requests, pair_list, pair_count):
    wave = waveform.reshape(STA, SAMPLES)
    pairs = jnp.swapaxes(pair_list, 1, 2).reshape(2, TILE)
    blocks, index = spectra(wave, requests, pairs, pair_count, forward)
    everything, indices = share(blocks, index)
    parts = crosses(everything, indices)
    stacked = collect(parts)
    return lags(stacked, lag)


def solution(mesh):
    forward, lag = wave_tables()
    in_specs = (P("pairs", "seg", None), P(), P("pairs", None, None), P("pairs"))
    out_specs = P(("pairs", "seg"), None)
    return jax.shard_map(
        functools.partial(body, forward, lag), mesh=mesh, in_specs=in_specs, out_specs=out_specs, check_vma=False
    )
```

```python
import functools
import math

import jax
import jax.numpy as jnp
import ml_dtypes
import numpy as np
from jax import lax
from jax.experimental import pallas as pl
from jax.experimental.pallas import tpu as pltpu
from jax.sharding import PartitionSpec as P

SAMPLES = 7680
K0 = 16
FB = 1024
HALF_WIN = 64
MAXLAG = 2560
LAGS = 5120
QUARTER = SAMPLES // 4
SUB = FB // 4
NZ, NX, NY, NC = 16, 4, 4, 2
STA = 32
TILE = 256
CHUNK = 640
DEAD = 4095
SLOTS = NC * STA
ROWS = NX * NZ * STA
VMEM_BYTES = 56 * 1024 * 1024
F32 = jnp.float32
BF16 = jnp.bfloat16
I32 = jnp.int32


def wave_tables():
    bins = np.concatenate([K0 + 4 * np.arange(SUB) + r for r in range(4)])
    phase = (np.arange(QUARTER)[:, None] * bins[None, :]) % SAMPLES
    angle = phase.astype(np.float32) * np.float32(2.0 * math.pi / SAMPLES)
    cos = np.cos(angle).astype(ml_dtypes.bfloat16)
    sin = np.sin(angle).astype(ml_dtypes.bfloat16)
    forward = np.stack([np.concatenate([cos[:, SUB * r : SUB * (r + 1)], sin[:, SUB * r : SUB * (r + 1)]], axis=1) for r in range(4)])
    lag = np.stack(
        [
            np.concatenate([cos[CHUNK * i : CHUNK * (i + 1)].T, sin[CHUNK * i : CHUNK * (i + 1)].T], axis=1)
            for i in range(QUARTER // CHUNK)
        ]
    )
    return forward, lag


def iota(shape, dim):
    return lax.broadcasted_iota(I32, shape, dim)


def where_am_i():
    tile = lax.axis_index("pairs")
    seg = lax.axis_index("seg")
    return tile // NX, tile % NX, seg // NC, seg % NC


def at(z, x, y, c):
    return (z * NX + x, y * NC + c)


def row_of_station(station):
    owner = lax.shift_right_logical(station, 5)
    return (owner & 3) * (NZ * STA) + lax.shift_right_logical(owner, 2) * STA + (station & 31)


def signal_all(peers):
    barrier = pltpu.get_barrier_semaphore()
    for peer in peers:
        pl.semaphore_signal(barrier, inc=1, device_id=peer, device_id_type=pl.DeviceIdType.MESH)


def remote(src, dst, send, recv, peer):
    return pltpu.make_async_remote_copy(
        src_ref=src, dst_ref=dst, send_sem=send, recv_sem=recv, device_id=peer, device_id_type=pl.DeviceIdType.MESH
    )


def pair_rows(count_ref, requests_ref, pairs_ref):
    tile = lax.axis_index("pairs")
    wanted = requests_ref[pl.ds(tile, 1), :].astype(F32)
    eye = iota((TILE, TILE), 0) == iota((TILE, TILE), 1)
    wanted_col = jnp.sum(jnp.where(eye, wanted, 0.0), axis=1, keepdims=True)
    ends = []
    for end in range(2):
        hit = iota((TILE, TILE), 0) == pairs_ref[end : end + 1, :]
        station = jnp.sum(jnp.where(hit, wanted_col, 0.0), axis=0, keepdims=True).astype(I32)
        ends.append(row_of_station(station))
    live = iota((1, TILE), 1) < count_ref[0]
    return jnp.where(live, ends[0] * 4096 + ends[1], DEAD * 4096 + DEAD)


def spectrum_part(wave_ref, table, r):
    def quarter(i):
        return wave_ref[:, QUARTER * i : QUARTER * (i + 1)].astype(F32)

    def times_table(lhs):
        return jnp.dot(lhs.astype(BF16), table[...], preferred_element_type=F32)

    if r % 2 == 0:
        sign = 1.0 - r
        out = times_table((quarter(0) + quarter(2)) + sign * (quarter(1) + quarter(3)))
        return out[:, :SUB], -out[:, SUB:]
    sign = r - 2.0
    out = times_table(jnp.concatenate([quarter(0) - quarter(2), quarter(1) - quarter(3)], axis=0))
    a_cos, a_sin = out[:STA, :SUB], out[:STA, SUB:]
    b_cos, b_sin = out[STA:, :SUB], out[STA:, SUB:]
    return a_cos + sign * b_sin, sign * b_cos - a_sin


def whiten(spec, block_ref):
    power = jnp.concatenate([re * re + im * im for re, im in spec], axis=0)
    high = power.astype(BF16)
    low = (power - high.astype(F32)).astype(BF16)
    parts = jnp.concatenate([high, low], axis=0)
    apart = iota((SUB, SUB), 0) - iota((SUB, SUB), 1)

    def band(lowest, highest):
        near = jnp.where((apart >= lowest) & (apart <= highest), 1.0, 0.0).astype(BF16)
        both = jnp.dot(parts, near, preferred_element_type=F32)
        return both[: 4 * STA] + both[4 * STA :]

    same = band(-16, 16)
    after = band(-15, 16)
    before = band(-16, 15)
    lane = iota((STA, 128), 1)
    for r in range(4):
        total = same[STA * r : STA * (r + 1)]
        for other in range(4):
            if other < r:
                total = total + after[STA * other : STA * (other + 1)]
            elif other > r:
                total = total + before[STA * other : STA * (other + 1)]
        j = 4 * iota((STA, SUB), 1) + r
        count = jnp.minimum(j + HALF_WIN, FB - 1) - jnp.maximum(j - HALF_WIN, 0) + 1
        scale = lax.rsqrt(total / count.astype(F32) + 1e-6)
        re = spec[r][0] * scale
        im = spec[r][1] * scale
        for g in range(2):
            re_g, im_g = re[:, 128 * g : 128 * (g + 1)], im[:, 128 * g : 128 * (g + 1)]
            block = 4 * r + 2 * g
            block_ref[block] = jnp.where(lane < 64, re_g, pltpu.roll(im_g, 64, 1)).astype(BF16)
            block_ref[block + 1] = jnp.where(lane < 64, pltpu.roll(re_g, 64, 1), im_g).astype(BF16)


def one_hot(indices_ref, hot_ref, group, y):
    pick = iota((SLOTS, TILE), 1) == iota((SLOTS, TILE), 0) + SLOTS * y
    firsts, seconds = [], []
    for k in range(4):
        packed = indices_ref[4 * group + k]
        first = lax.shift_right_logical(packed, 12).astype(F32)
        second = (packed & 4095).astype(F32)
        firsts.append(jnp.sum(jnp.where(pick, first, 0.0), axis=1, keepdims=True))
        seconds.append(jnp.sum(jnp.where(pick, second, 0.0), axis=1, keepdims=True))
    rows = jnp.concatenate(firsts + seconds, axis=0).astype(I32)
    hot_ref[group] = jnp.where(iota((8 * SLOTS, ROWS), 1) == rows, 1.0, 0.0).astype(BF16)


def cross_group(hot, all_ref, part_ref, group):
    both = jnp.dot(hot, all_ref[...], preferred_element_type=F32)
    straight, turned = 0.0, 0.0
    for s in range(NY):
        first = both[: 4 * SLOTS, 128 * s : 128 * (s + 1)]
        second = both[4 * SLOTS :, 128 * s : 128 * (s + 1)]
        straight = straight + first * second
        turned = turned + first * pltpu.roll(second, 64, 1)
    lane = iota((4 * SLOTS, 128), 1)
    value = jnp.where(lane < 64, straight + pltpu.roll(straight, 64, 1), turned - pltpu.roll(turned, 64, 1))
    for k in range(4):
        for core in range(NC):
            part_ref[core, 4 * group + k] = value[SLOTS * k + STA * core : SLOTS * k + STA * (core + 1)]


FAR_FIRST = (8, 7, 9, 6, 10, 5, 11, 4, 12, 3, 13, 2, 14, 1, 15)


def whole_kernel(
    count_ref,
    wave_ref,
    requests_ref,
    pairs_ref,
    forward_ref,
    lag_ref,
    out_ref,
    forward,
    lag,
    block_ref,
    index_ref,
    all_ref,
    indices_ref,
    hot_ref,
    part_ref,
    other_ref,
    stack_ref,
    final_ref,
    table_sem,
    z_send,
    z_recv,
    i_send,
    i_recv,
    xy_send,
    xy_recv,
    c_send,
    c_recv,
    b_send,
    b_recv,
):
    z, x, y, c = where_am_i()
    z_peer = [at((z + d) % NZ, x, y, c) for d in range(1, NZ)]
    x_peer = [at(z, (x + d) % NX, y, c) for d in range(1, NX)]
    y_peer = [at(z, x, (y + d) % NY, c) for d in range(1, NY)]
    partner = at(z, x, y, 1 - c)
    peers = z_peer + x_peer + y_peer + [partner]
    signal_all(peers)

    tables = [pltpu.make_async_copy(forward_ref.at[r], forward.at[r], table_sem.at[r]) for r in range(4)]
    tables.append(pltpu.make_async_copy(lag_ref, lag, table_sem.at[4]))
    for copy in tables:
        copy.start()
    index_ref[0] = pair_rows(count_ref, requests_ref, pairs_ref)
    spec = []
    for r in range(4):
        tables[r].wait()
        spec.append(spectrum_part(wave_ref, forward.at[r], r))
    whiten(spec, block_ref)

    pl.semaphore_wait(pltpu.get_barrier_semaphore(), len(peers))

    def part(half, xs, ys):
        rows = pl.ds(pl.multiple_of(xs * (NZ * STA) + half * (NZ * STA // 2), 256), NZ * STA // 2)
        return all_ref.at[rows, pl.ds(pl.multiple_of(ys * 128, 128), 128)]

    def rows_of(zs):
        rows = pl.ds(pl.multiple_of(x * (NZ * STA) + zs * STA, STA), STA)
        return all_ref.at[rows, pl.ds(pl.multiple_of(y * 128, 128), 128)]

    sent = []
    for d in FAR_FIRST:
        copy = remote(index_ref.at[0], indices_ref.at[z], i_send.at[d], i_recv.at[z], z_peer[d - 1])
        copy.start()
        sent.append(copy)
        copy = remote(block_ref.at[(z + d) % NZ], rows_of(z), z_send.at[d], z_recv.at[z], z_peer[d - 1])
        copy.start()
        sent.append(copy)
    all_ref[pl.ds(pl.multiple_of(x * (NZ * STA) + z * STA, STA), STA), pl.ds(pl.multiple_of(y * 128, 128), 128)] = (
        block_ref[z]
    )
    indices_ref[z] = index_ref[0]

    for d in range(1, NZ):
        zs = (z + d) % NZ
        remote(index_ref.at[0], indices_ref.at[zs], i_send.at[0], i_recv.at[zs], z_peer[0]).wait_recv()

    def hot_group(group, carry):
        one_hot(indices_ref, hot_ref, group, y)
        return carry

    lax.fori_loop(0, 4, hot_group, 0)

    def arrived(half):
        for k in range(NZ // 2):
            zs = half * (NZ // 2) + k

            @pl.when(zs != z)
            def _():
                remote(block_ref.at[0], rows_of(zs), z_send.at[0], z_recv.at[zs], z_peer[0]).wait_recv()

    counter = [0]

    def give(half, xs, ys, to):
        for peer in to:
            ref = part(half, xs, ys)
            copy = remote(ref, ref, xy_send.at[counter[0]], xy_recv.at[half, xs, ys], peer)
            counter[0] += 1
            copy.start()
            sent.append(copy)

    def take(half, xs, ys):
        ref = part(half, xs, ys)
        remote(ref, ref, xy_send.at[0], xy_recv.at[half, xs, ys], z_peer[0]).wait_recv()

    arrived(0)
    give(0, x, y, x_peer + y_peer)
    arrived(1)
    give(1, x, y, y_peer + x_peer)
    for d in (1, 3, 2):
        xs, ys = (x + d) % NX, (y + d) % NY
        take(0, xs, y)
        give(0, xs, y, y_peer)
        take(1, x, ys)
        give(1, x, ys, x_peer)
    for d in range(1, NX):
        xs, ys = (x + d) % NX, (y + d) % NY
        take(0, x, ys)
        take(1, xs, y)
        for e in range(1, NY):
            take(0, xs, (y + e) % NY)
            take(1, (x + e) % NX, ys)

    def swap(group):
        return remote(
            part_ref.at[1 - c, pl.ds(4 * group, 4)],
            other_ref.at[pl.ds(4 * group, 4)],
            c_send.at[group],
            c_recv.at[group],
            partner,
        )

    def back(to):
        return remote(stack_ref.at[to], final_ref.at[z], b_send.at[to], b_recv.at[z], at(to, x, y, c))

    def finish(group):
        swap(group).wait_recv()
        for k in range(4):
            to = 4 * group + k
            stack_ref[to] = (part_ref[c, to] + other_ref[to]).astype(BF16)

            @pl.when(to != z)
            def _():
                back(to).start()

    def group_step(group, carry):
        cross_group(hot_ref[group], all_ref, part_ref, group)
        swap(group).start()

        @pl.when(group > 0)
        def _():
            finish(group - 1)

        return carry

    lax.fori_loop(0, 4, group_step, 0)
    finish(3)
    final_ref[z] = stack_ref[z]
    for d in range(1, NZ):
        zs = (z + d) % NZ
        remote(stack_ref.at[0], final_ref.at[zs], b_send.at[0], b_recv.at[zs], z_peer[0]).wait_recv()
    tables[4].wait()
    stack = [final_ref[k] for k in range(NZ)]
    for chunk in range(QUARTER // CHUNK):
        lag_chunk(stack, lag.at[chunk], out_ref, chunk)
    for copy in sent:
        copy.wait_send()
    for group in range(4):
        swap(group).wait_send()
    for d in range(1, NZ):
        back((z + d) % NZ).wait_send()


def whole(count, wave, requests, pairs, forward, lag):
    dma = pltpu.SemaphoreType.DMA
    vmem = pl.BlockSpec(memory_space=pltpu.VMEM)
    return pl.pallas_call(
        whole_kernel,
        out_shape=jax.ShapeDtypeStruct((STA, LAGS), F32),
        in_specs=[pl.BlockSpec(memory_space=pltpu.SMEM), vmem, vmem, vmem] + [pl.BlockSpec(memory_space=pl.ANY)] * 2,
        out_specs=vmem,
        scratch_shapes=[
            pltpu.VMEM(forward.shape, BF16),
            pltpu.VMEM(lag.shape, BF16),
            pltpu.VMEM((NZ, STA, 128), BF16),
            pltpu.VMEM((1, 1, TILE), I32),
            pltpu.VMEM((ROWS, NY * 128), BF16),
            pltpu.VMEM((NZ, 1, TILE), I32),
            pltpu.VMEM((4, 8 * SLOTS, ROWS), BF16),
            pltpu.VMEM((NC, NZ, STA, 128), F32),
            pltpu.VMEM((NZ, STA, 128), F32),
            pltpu.VMEM((NZ, STA, 128), BF16),
            pltpu.VMEM((NZ, STA, 128), BF16),
            dma((5,)),
            dma((NZ,)),
            dma((NZ,)),
            dma((NZ,)),
            dma((NZ,)),
            dma((2 * (NX * NY - 1),)),
            dma((2, NX, NY)),
            dma((4,)),
            dma((4,)),
            dma((NZ,)),
            dma((NZ,)),
        ],
        compiler_params=pltpu.CompilerParams(collective_id=0, has_side_effects=True, vmem_limit_bytes=VMEM_BYTES),
        name="whole",
    )(count, wave, requests, pairs, forward, lag)


def lag_chunk(stack, table, out_ref, chunk):
    lane = iota((STA, 128), 1)
    sides = []
    for r in range(4):
        re, im = [], []
        for g in range(2):
            one = stack[4 * r + 2 * g].astype(F32)
            two = stack[4 * r + 2 * g + 1].astype(F32)
            re.append(jnp.where(lane < 64, one, pltpu.roll(two, 64, 1)))
            im.append(jnp.where(lane < 64, pltpu.roll(one, 64, 1), two))
        sides.append((jnp.concatenate(re, axis=1).astype(BF16), jnp.concatenate(im, axis=1).astype(BF16)))

    def dot(lhs, r, sine):
        rows = slice(SUB * r, SUB * (r + 1))
        return jnp.dot(lhs, table[rows, CHUNK * sine : CHUNK * (sine + 1)], preferred_element_type=F32)

    even, odd = [], []
    for r in (0, 2):
        even.append(dot(sides[r][0], r, 0) - dot(sides[r][1], r, 1))
    for r in (1, 3):
        lhs = jnp.concatenate(sides[r], axis=0)
        cos, sin = dot(lhs, r, 0), dot(lhs, r, 1)
        odd.append((cos[:STA] - sin[STA:], sin[:STA] + cos[STA:]))
    scale = 1.0 / math.sqrt(FB * NY * NC)
    plus, minus = (even[0] + even[1]) * scale, (even[0] - even[1]) * scale
    real = (odd[0][0] + odd[1][0]) * scale
    imag = (odd[0][1] - odd[1][1]) * scale

    def put(turns, value):
        lag = MAXLAG + QUARTER * turns + CHUNK * chunk
        if 0 <= lag < LAGS:
            out_ref[:, lag : lag + CHUNK] = value

    put(0, plus + real)
    put(-2, plus - real)
    put(1, minus - imag)
    put(-1, minus + imag)


def body(forward, lag, waveform, requests, pair_list, pair_count):
    wave = waveform.reshape(STA, SAMPLES)
    pairs = jnp.swapaxes(pair_list, 1, 2).reshape(2, TILE)
    return whole(pair_count, wave, requests, pairs, forward, lag)


def solution(mesh):
    forward, lag = wave_tables()
    in_specs = (P("pairs", "seg", None), P(), P("pairs", None, None), P("pairs"))
    out_specs = P(("pairs", "seg"), None)
    return jax.shard_map(
        functools.partial(body, forward, lag), mesh=mesh, in_specs=in_specs, out_specs=out_specs, check_vma=False
    )
```

```python
import functools
import math

import jax
import jax.numpy as jnp
import ml_dtypes
import numpy as np
from jax import lax
from jax.experimental import pallas as pl
from jax.experimental.pallas import tpu as pltpu
from jax.sharding import PartitionSpec as P

SAMPLES = 7680
K0 = 16
FB = 1024
HALF_WIN = 64
MAXLAG = 2560
LAGS = 5120
QUARTER = SAMPLES // 4
SUB = FB // 4
NZ, NX, NY, NC = 16, 4, 4, 2
STA = 32
TILE = 256
CHUNK = 640
DEAD = 4095
SLOTS = NC * STA
ROWS = NX * NZ * STA
HALF_ROWS = ROWS // 2
NEAR = 4
VMEM_BYTES = 56 * 1024 * 1024
F32 = jnp.float32
BF16 = jnp.bfloat16
I32 = jnp.int32


def wave_tables():
    bins = np.concatenate([K0 + 4 * np.arange(SUB) + r for r in range(4)])
    phase = (np.arange(QUARTER)[:, None] * bins[None, :]) % SAMPLES
    angle = phase.astype(np.float32) * np.float32(2.0 * math.pi / SAMPLES)
    cos = np.cos(angle).astype(ml_dtypes.bfloat16)
    sin = np.sin(angle).astype(ml_dtypes.bfloat16)
    forward = np.stack([np.concatenate([cos[:, SUB * r : SUB * (r + 1)], sin[:, SUB * r : SUB * (r + 1)]], axis=1) for r in range(4)])
    lag = np.stack(
        [
            np.concatenate([cos[CHUNK * i : CHUNK * (i + 1)].T, sin[CHUNK * i : CHUNK * (i + 1)].T], axis=1)
            for i in range(QUARTER // CHUNK)
        ]
    )
    return forward, lag


def iota(shape, dim):
    return lax.broadcasted_iota(I32, shape, dim)


def where_am_i():
    tile = lax.axis_index("pairs")
    seg = lax.axis_index("seg")
    return tile // NX, tile % NX, seg // NC, seg % NC


def at(z, x, y, c):
    return (z * NX + x, y * NC + c)


def row_of_station(station, z):
    owner = lax.shift_right_logical(station, 5)
    away = (lax.shift_right_logical(owner, 2) - z + NEAR) & (NZ - 1)
    row = lax.shift_right_logical(away, 3) * HALF_ROWS + (owner & 3) * (8 * STA) + (away & 7) * STA + (station & 31)
    return jnp.where(station == DEAD, -1, row)


def signal_all(peers):
    barrier = pltpu.get_barrier_semaphore()
    for peer in peers:
        pl.semaphore_signal(barrier, inc=1, device_id=peer, device_id_type=pl.DeviceIdType.MESH)


def remote(src, dst, send, recv, peer):
    return pltpu.make_async_remote_copy(
        src_ref=src, dst_ref=dst, send_sem=send, recv_sem=recv, device_id=peer, device_id_type=pl.DeviceIdType.MESH
    )


def pair_rows(count_ref, requests_ref, pairs_ref):
    tile = lax.axis_index("pairs")
    wanted = requests_ref[pl.ds(tile, 1), :].astype(F32)
    eye = iota((TILE, TILE), 0) == iota((TILE, TILE), 1)
    wanted_col = jnp.sum(jnp.where(eye, wanted, 0.0), axis=1, keepdims=True)
    ends = []
    for end in range(2):
        hit = iota((TILE, TILE), 0) == pairs_ref[end : end + 1, :]
        station = jnp.sum(jnp.where(hit, wanted_col, 0.0), axis=0, keepdims=True).astype(I32)
        ends.append(station)
    live = iota((1, TILE), 1) < count_ref[0]
    return jnp.where(live, ends[0] * 4096 + ends[1], DEAD * 4096 + DEAD)


def spectrum_part(wave_ref, table, r):
    def quarter(i):
        return wave_ref[:, QUARTER * i : QUARTER * (i + 1)].astype(F32)

    def times_table(lhs):
        return jnp.dot(lhs.astype(BF16), table[...], preferred_element_type=F32)

    if r % 2 == 0:
        sign = 1.0 - r
        out = times_table((quarter(0) + quarter(2)) + sign * (quarter(1) + quarter(3)))
        return out[:, :SUB], -out[:, SUB:]
    sign = r - 2.0
    out = times_table(jnp.concatenate([quarter(0) - quarter(2), quarter(1) - quarter(3)], axis=0))
    a_cos, a_sin = out[:STA, :SUB], out[:STA, SUB:]
    b_cos, b_sin = out[STA:, :SUB], out[STA:, SUB:]
    return a_cos + sign * b_sin, sign * b_cos - a_sin


def whiten(spec, block_ref):
    power = jnp.concatenate([re * re + im * im for re, im in spec], axis=0)
    high = power.astype(BF16)
    low = (power - high.astype(F32)).astype(BF16)
    parts = jnp.concatenate([high, low], axis=0)
    apart = iota((SUB, SUB), 0) - iota((SUB, SUB), 1)

    def band(lowest, highest):
        near = jnp.where((apart >= lowest) & (apart <= highest), 1.0, 0.0).astype(BF16)
        both = jnp.dot(parts, near, preferred_element_type=F32)
        return both[: 4 * STA] + both[4 * STA :]

    same = band(-16, 16)
    after = band(-15, 16)
    before = band(-16, 15)
    lane = iota((STA, 128), 1)
    for r in range(4):
        total = same[STA * r : STA * (r + 1)]
        for other in range(4):
            if other < r:
                total = total + after[STA * other : STA * (other + 1)]
            elif other > r:
                total = total + before[STA * other : STA * (other + 1)]
        j = 4 * iota((STA, SUB), 1) + r
        count = jnp.minimum(j + HALF_WIN, FB - 1) - jnp.maximum(j - HALF_WIN, 0) + 1
        scale = lax.rsqrt(total / count.astype(F32) + 1e-6)
        re = spec[r][0] * scale
        im = spec[r][1] * scale
        for g in range(2):
            re_g, im_g = re[:, 128 * g : 128 * (g + 1)], im[:, 128 * g : 128 * (g + 1)]
            block = 4 * r + 2 * g
            block_ref[block] = jnp.where(lane < 64, re_g, pltpu.roll(im_g, 64, 1)).astype(BF16)
            block_ref[block + 1] = jnp.where(lane < 64, pltpu.roll(re_g, 64, 1), im_g).astype(BF16)


def distance(group, k):
    turn = 2 * group + (k + 1) // 2
    return 8 - turn if k % 2 else 8 + turn


def one_hot(indices_ref, hot_ref, group, z, y):
    pick = iota((SLOTS, TILE), 1) == iota((SLOTS, TILE), 0) + SLOTS * y
    firsts, seconds = [], []
    for k in range(4):
        packed = indices_ref[(z + distance(group, k)) % NZ]
        first = row_of_station(lax.shift_right_logical(packed, 12), z).astype(F32)
        second = row_of_station(packed & 4095, z).astype(F32)
        firsts.append(jnp.sum(jnp.where(pick, first, 0.0), axis=1, keepdims=True))
        seconds.append(jnp.sum(jnp.where(pick, second, 0.0), axis=1, keepdims=True))
    rows = jnp.concatenate(firsts + seconds, axis=0).astype(I32)
    for far in range(2):
        column = iota((8 * SLOTS, HALF_ROWS), 1) + far * HALF_ROWS
        hot_ref[far, group] = jnp.where(column == rows, 1.0, 0.0).astype(BF16)


def cross_group(both, part_ref, group):
    straight, turned = 0.0, 0.0
    for s in range(NY):
        first = both[: 4 * SLOTS, 128 * s : 128 * (s + 1)]
        second = both[4 * SLOTS :, 128 * s : 128 * (s + 1)]
        straight = straight + first * second
        turned = turned + first * pltpu.roll(second, 64, 1)
    lane = iota((4 * SLOTS, 128), 1)
    value = jnp.where(lane < 64, straight + pltpu.roll(straight, 64, 1), turned - pltpu.roll(turned, 64, 1))
    for k in range(4):
        for core in range(NC):
            part_ref[core, 4 * group + k] = value[SLOTS * k + STA * core : SLOTS * k + STA * (core + 1)]


SEND_ORDER = (4, 12, 3, 13, 2, 14, 1, 15, 8, 7, 9, 6, 10, 5, 11)


def whole_kernel(
    count_in,
    wave_in,
    requests_in,
    pairs_in,
    forward_ref,
    lag_ref,
    out_ref,
    count_ref,
    wave_ref,
    requests_ref,
    pairs_ref,
    forward,
    lag,
    block_ref,
    index_ref,
    all_ref,
    indices_ref,
    hot_ref,
    near_ref,
    part_ref,
    other_ref,
    stack_ref,
    final_ref,
    input_sem,
    table_sem,
    z_send,
    z_recv,
    i_send,
    i_recv,
    xy_send,
    xy_recv,
    c_send,
    c_recv,
    b_send,
    b_recv,
):
    z, x, y, c = where_am_i()
    z_peer = [at((z + d) % NZ, x, y, c) for d in range(NZ)]
    x_peer = [at(z, (x + d) % NX, y, c) for d in (2, 1, 3)]
    y_peer = [at(z, x, (y + d) % NY, c) for d in (2, 1, 3)]
    partner = at(z, x, y, 1 - c)
    peers = z_peer[1:] + x_peer + y_peer + [partner]

    inputs = [
        pltpu.make_async_copy(src, dst, input_sem.at[k])
        for k, (src, dst) in enumerate(
            ((wave_in, wave_ref), (requests_in, requests_ref), (pairs_in, pairs_ref), (count_in, count_ref))
        )
    ]
    tables = [pltpu.make_async_copy(forward_ref.at[r], forward.at[r], table_sem.at[r]) for r in range(4)]
    tables.append(pltpu.make_async_copy(lag_ref, lag, table_sem.at[4]))
    inputs[0].start()
    tables[0].start()
    tables[1].start()
    for copy in inputs[1:]:
        copy.start()
    signal_all(peers)
    inputs[0].wait()
    spec = []
    for r in range(4):
        tables[r].wait()
        if r < 2:
            tables[r + 2].start()
        spec.append(spectrum_part(wave_ref, forward.at[r], r))
    whiten(spec, block_ref)

    pl.semaphore_wait(pltpu.get_barrier_semaphore(), len(peers))

    def lanes(ys):
        return pl.ds(pl.multiple_of(ys * 128, 128), 128)

    def rows_of(d):
        away = (d + NEAR) % NZ
        return pl.ds(pl.multiple_of(away // 8 * HALF_ROWS + x * (8 * STA) + away % 8 * STA, STA), STA)

    def part(far, sub, xs, ys):
        rows = pl.ds(pl.multiple_of(far * HALF_ROWS + xs * (8 * STA) + sub * (4 * STA), 4 * STA), 4 * STA)
        return all_ref.at[rows, lanes(ys)]

    sent = []
    for d in SEND_ORDER:
        there = all_ref.at[rows_of(-d), lanes(y)]
        copy = remote(block_ref.at[(z + d) % NZ], there, z_send.at[d], z_recv.at[NZ - d], z_peer[d])
        copy.start()
        sent.append(copy)
    all_ref[rows_of(0), lanes(y)] = block_ref[z]

    def arrived(far, sub):
        for k in range(4):
            d = (8 * far + 4 * sub + k - NEAR) % NZ
            if d != 0:
                here = all_ref.at[rows_of(d), lanes(y)]
                remote(block_ref.at[0], here, z_send.at[0], z_recv.at[d], z_peer[1]).wait_recv()

    counter = [0]

    def give(far, sub, xs, ys, to):
        for peer in to:
            ref = part(far, sub, xs, ys)
            copy = remote(ref, ref, xy_send.at[counter[0]], xy_recv.at[2 * far + sub, xs, ys], peer)
            counter[0] += 1
            copy.start()
            sent.append(copy)

    def take(far, sub, xs, ys):
        ref = part(far, sub, xs, ys)
        remote(ref, ref, xy_send.at[0], xy_recv.at[2 * far + sub, xs, ys], z_peer[1]).wait_recv()

    def begin(far):
        arrived(far, 0)
        give(far, 0, x, y, x_peer)
        arrived(far, 1)
        give(far, 1, x, y, y_peer)
        give(far, 0, x, y, y_peer)
        give(far, 1, x, y, x_peer)

    def forward_on(far):
        for d in (3, 1, 2):
            xs, ys = (x + d) % NX, (y + d) % NY
            take(far, 0, xs, y)
            give(far, 0, xs, y, y_peer)
            take(far, 1, x, ys)
            give(far, 1, x, ys, x_peer)

    def settle(far):
        for d in (1, 3, 2):
            xs, ys = (x + d) % NX, (y + d) % NY
            take(far, 0, x, ys)
            take(far, 1, xs, y)
            for e in (1, 3, 2):
                take(far, 0, xs, (y + e) % NY)
                take(far, 1, (x + e) % NX, ys)

    for copy in inputs[1:]:
        copy.wait()
    index_ref[0] = pair_rows(count_ref, requests_ref, pairs_ref)
    begin(0)
    begin(1)
    for d in SEND_ORDER:
        copy = remote(index_ref.at[0], indices_ref.at[z], i_send.at[d], i_recv.at[NZ - d], z_peer[d])
        copy.start()
        sent.append(copy)
    indices_ref[z] = index_ref[0]
    forward_on(0)
    for d in range(1, NZ):
        zs = (z + d) % NZ
        remote(index_ref.at[0], indices_ref.at[zs], i_send.at[0], i_recv.at[d], z_peer[1]).wait_recv()
    forward_on(1)

    def hot_group(group, carry):
        one_hot(indices_ref, hot_ref, group, z, y)
        return carry

    lax.fori_loop(0, 4, hot_group, 0)
    settle(0)

    def near_group(group, carry):
        near_ref[group] = jnp.dot(hot_ref[0, group], all_ref[:HALF_ROWS], preferred_element_type=F32)
        return carry

    tables[4].start()
    lax.fori_loop(0, 4, near_group, 0)
    settle(1)

    def swap(group):
        return remote(
            part_ref.at[1 - c, pl.ds(4 * group, 4)],
            other_ref.at[pl.ds(4 * group, 4)],
            c_send.at[group],
            c_recv.at[group],
            partner,
        )

    def back(group, k):
        d = distance(group, k)
        to = at((z + d) % NZ, x, y, c)
        return remote(stack_ref.at[4 * group + k], final_ref.at[z], b_send.at[4 * group + k], b_recv.at[(NZ - d) % NZ], to)

    def finish(group):
        swap(group).wait_recv()
        for k in range(4):
            place = 4 * group + k
            stack_ref[place] = (part_ref[c, place] + other_ref[place]).astype(BF16)
            if k < 3:
                back(group, k).start()
            else:

                @pl.when(group < 3)
                def _():
                    back(group, k).start()

    def group_step(group, carry):
        far = jnp.dot(hot_ref[1, group], all_ref[HALF_ROWS:], preferred_element_type=F32)
        cross_group(near_ref[group] + far, part_ref, group)
        swap(group).start()

        @pl.when(group > 0)
        def _():
            finish(group - 1)

        return carry

    lax.fori_loop(0, 4, group_step, 0)
    finish(3)
    final_ref[z] = stack_ref[NZ - 1]
    for d in range(1, NZ):
        here = final_ref.at[(z + d) % NZ]
        remote(stack_ref.at[0], here, b_send.at[0], b_recv.at[d], z_peer[1]).wait_recv()
    tables[4].wait()
    stack = [final_ref[k] for k in range(NZ)]
    for chunk in range(QUARTER // CHUNK):
        lag_chunk(stack, lag.at[chunk], out_ref, chunk)
    for copy in sent:
        copy.wait_send()
    for group in range(4):
        swap(group).wait_send()
    for place in range(NZ - 1):
        back(place // 4, place % 4).wait_send()


def whole(count, wave, requests, pairs, forward, lag):
    dma = pltpu.SemaphoreType.DMA
    vmem = pl.BlockSpec(memory_space=pltpu.VMEM)
    return pl.pallas_call(
        whole_kernel,
        out_shape=jax.ShapeDtypeStruct((STA, LAGS), F32),
        in_specs=[pl.BlockSpec(memory_space=pl.ANY)] * 6,
        out_specs=vmem,
        scratch_shapes=[
            pltpu.SMEM((1,), I32),
            pltpu.VMEM(wave.shape, BF16),
            pltpu.VMEM(requests.shape, I32),
            pltpu.VMEM(pairs.shape, I32),
            pltpu.VMEM(forward.shape, BF16),
            pltpu.VMEM(lag.shape, BF16),
            pltpu.VMEM((NZ, STA, 128), BF16),
            pltpu.VMEM((1, 1, TILE), I32),
            pltpu.VMEM((ROWS, NY * 128), BF16),
            pltpu.VMEM((NZ, 1, TILE), I32),
            pltpu.VMEM((2, 4, 8 * SLOTS, HALF_ROWS), BF16),
            pltpu.VMEM((4, 8 * SLOTS, NY * 128), F32),
            pltpu.VMEM((NC, NZ, STA, 128), F32),
            pltpu.VMEM((NZ, STA, 128), F32),
            pltpu.VMEM((NZ, STA, 128), BF16),
            pltpu.VMEM((NZ, STA, 128), BF16),
            dma((4,)),
            dma((5,)),
            dma((NZ,)),
            dma((NZ,)),
            dma((NZ,)),
            dma((NZ,)),
            dma((4 * (NX * NY - 1),)),
            dma((4, NX, NY)),
            dma((4,)),
            dma((4,)),
            dma((NZ,)),
            dma((NZ,)),
        ],
        compiler_params=pltpu.CompilerParams(collective_id=0, has_side_effects=True, vmem_limit_bytes=VMEM_BYTES),
        name="whole",
    )(count, wave, requests, pairs, forward, lag)


def lag_chunk(stack, table, out_ref, chunk):
    lane = iota((STA, 128), 1)
    sides = []
    for r in range(4):
        re, im = [], []
        for g in range(2):
            one = stack[4 * r + 2 * g].astype(F32)
            two = stack[4 * r + 2 * g + 1].astype(F32)
            re.append(jnp.where(lane < 64, one, pltpu.roll(two, 64, 1)))
            im.append(jnp.where(lane < 64, pltpu.roll(one, 64, 1), two))
        sides.append((jnp.concatenate(re, axis=1).astype(BF16), jnp.concatenate(im, axis=1).astype(BF16)))

    def dot(lhs, r, sine):
        rows = slice(SUB * r, SUB * (r + 1))
        return jnp.dot(lhs, table[rows, CHUNK * sine : CHUNK * (sine + 1)], preferred_element_type=F32)

    even, odd = [], []
    for r in (0, 2):
        even.append(dot(sides[r][0], r, 0) - dot(sides[r][1], r, 1))
    for r in (1, 3):
        lhs = jnp.concatenate(sides[r], axis=0)
        cos, sin = dot(lhs, r, 0), dot(lhs, r, 1)
        odd.append((cos[:STA] - sin[STA:], sin[:STA] + cos[STA:]))
    plus, minus = even[0] + even[1], even[0] - even[1]
    real = odd[0][0] + odd[1][0]
    imag = odd[0][1] - odd[1][1]

    def put(turns, value):
        lag = MAXLAG + QUARTER * turns + CHUNK * chunk
        if 0 <= lag < LAGS:
            out_ref[:, lag : lag + CHUNK] = value

    put(0, plus + real)
    put(-2, plus - real)
    put(1, minus - imag)
    put(-1, minus + imag)


def body(forward, lag, waveform, requests, pair_list, pair_count):
    wave = waveform.reshape(STA, SAMPLES)
    pairs = jnp.swapaxes(pair_list, 1, 2).reshape(2, TILE)
    return whole(pair_count, wave, requests, pairs, forward, lag) * (1.0 / math.sqrt(FB * NY * NC))


def solution(mesh):
    forward, lag = wave_tables()
    in_specs = (P("pairs", "seg", None), P(), P("pairs", None, None), P("pairs"))
    out_specs = P(("pairs", "seg"), None)
    return jax.shard_map(
        functools.partial(body, forward, lag), mesh=mesh, in_specs=in_specs, out_specs=out_specs, check_vma=False
    )
```

```python
import functools
import math

import jax
import jax.numpy as jnp
import ml_dtypes
import numpy as np
from jax import lax
from jax.experimental import pallas as pl
from jax.experimental.pallas import tpu as pltpu
from jax.sharding import PartitionSpec as P

SAMPLES = 7680
K0 = 16
FB = 1024
HALF_WIN = 64
MAXLAG = 2560
LAGS = 5120
QUARTER = SAMPLES // 4
SUB = FB // 4
NZ, NX, NY, NC = 16, 4, 4, 2
STA = 32
TILE = 256
CHUNK = 640
DEAD = 4095
SLOTS = NC * STA
ROWS = NX * NZ * STA
HALF_ROWS = ROWS // 2
NEAR = 4
VMEM_BYTES = 54 * 1024 * 1024
LAGS_VMEM_BYTES = 20 * 1024 * 1024
F32 = jnp.float32
BF16 = jnp.bfloat16
I32 = jnp.int32


def wave_tables():
    bins = np.concatenate([K0 + 4 * np.arange(SUB) + r for r in range(4)])
    phase = (np.arange(QUARTER)[:, None] * bins[None, :]) % SAMPLES
    angle = phase.astype(np.float32) * np.float32(2.0 * math.pi / SAMPLES)
    cos = np.cos(angle).astype(ml_dtypes.bfloat16)
    sin = np.sin(angle).astype(ml_dtypes.bfloat16)
    forward = np.stack([np.concatenate([cos[:, SUB * r : SUB * (r + 1)], sin[:, SUB * r : SUB * (r + 1)]], axis=1) for r in range(4)])
    lag = np.stack(
        [
            np.concatenate([cos[CHUNK * i : CHUNK * (i + 1)].T, sin[CHUNK * i : CHUNK * (i + 1)].T], axis=1)
            for i in range(QUARTER // CHUNK)
        ]
    )
    return forward, lag


def iota(shape, dim):
    return lax.broadcasted_iota(I32, shape, dim)


def where_am_i():
    tile = lax.axis_index("pairs")
    seg = lax.axis_index("seg")
    return tile // NX, tile % NX, seg // NC, seg % NC


def at(z, x, y, c):
    return (z * NX + x, y * NC + c)


def row_of_station(station, z):
    owner = lax.shift_right_logical(station, 5)
    away = (lax.shift_right_logical(owner, 2) - z + NEAR) & (NZ - 1)
    row = lax.shift_right_logical(away, 3) * HALF_ROWS + (owner & 3) * (8 * STA) + (away & 7) * STA + (station & 31)
    return jnp.where(station == DEAD, -1, row)


def signal_all(peers):
    barrier = pltpu.get_barrier_semaphore()
    for peer in peers:
        pl.semaphore_signal(barrier, inc=1, device_id=peer, device_id_type=pl.DeviceIdType.MESH)


def remote(src, dst, send, recv, peer):
    return pltpu.make_async_remote_copy(
        src_ref=src, dst_ref=dst, send_sem=send, recv_sem=recv, device_id=peer, device_id_type=pl.DeviceIdType.MESH
    )


def pair_rows(count_ref, requests_ref, pairs_ref):
    tile = lax.axis_index("pairs")
    wanted = requests_ref[pl.ds(tile, 1), :].astype(F32)
    eye = iota((TILE, TILE), 0) == iota((TILE, TILE), 1)
    wanted_col = jnp.sum(jnp.where(eye, wanted, 0.0), axis=1, keepdims=True)
    ends = []
    for end in range(2):
        hit = iota((TILE, TILE), 0) == pairs_ref[end : end + 1, :]
        station = jnp.sum(jnp.where(hit, wanted_col, 0.0), axis=0, keepdims=True).astype(I32)
        ends.append(station)
    live = iota((1, TILE), 1) < count_ref[0]
    return jnp.where(live, ends[0] * 4096 + ends[1], DEAD * 4096 + DEAD)


def spectrum_part(wave_ref, table, r):
    def quarter(i):
        return wave_ref[:, QUARTER * i : QUARTER * (i + 1)].astype(F32)

    def times_table(lhs):
        return jnp.dot(lhs.astype(BF16), table[...], preferred_element_type=F32)

    if r % 2 == 0:
        sign = 1.0 - r
        out = times_table((quarter(0) + quarter(2)) + sign * (quarter(1) + quarter(3)))
        return out[:, :SUB], -out[:, SUB:]
    sign = r - 2.0
    out = times_table(jnp.concatenate([quarter(0) - quarter(2), quarter(1) - quarter(3)], axis=0))
    a_cos, a_sin = out[:STA, :SUB], out[:STA, SUB:]
    b_cos, b_sin = out[STA:, :SUB], out[STA:, SUB:]
    return a_cos + sign * b_sin, sign * b_cos - a_sin


def whiten(spec, block_ref):
    power = jnp.concatenate([re * re + im * im for re, im in spec], axis=0)
    high = power.astype(BF16)
    low = (power - high.astype(F32)).astype(BF16)
    parts = jnp.concatenate([high, low], axis=0)
    apart = iota((SUB, SUB), 0) - iota((SUB, SUB), 1)

    def band(lowest, highest):
        near = jnp.where((apart >= lowest) & (apart <= highest), 1.0, 0.0).astype(BF16)
        both = jnp.dot(parts, near, preferred_element_type=F32)
        return both[: 4 * STA] + both[4 * STA :]

    same = band(-16, 16)
    after = band(-15, 16)
    before = band(-16, 15)
    lane = iota((STA, 128), 1)
    for r in range(4):
        total = same[STA * r : STA * (r + 1)]
        for other in range(4):
            if other < r:
                total = total + after[STA * other : STA * (other + 1)]
            elif other > r:
                total = total + before[STA * other : STA * (other + 1)]
        j = 4 * iota((STA, SUB), 1) + r
        count = jnp.minimum(j + HALF_WIN, FB - 1) - jnp.maximum(j - HALF_WIN, 0) + 1
        scale = lax.rsqrt(total / count.astype(F32) + 1e-6)
        re = spec[r][0] * scale
        im = spec[r][1] * scale
        for g in range(2):
            re_g, im_g = re[:, 128 * g : 128 * (g + 1)], im[:, 128 * g : 128 * (g + 1)]
            block = 4 * r + 2 * g
            block_ref[block] = jnp.where(lane < 64, re_g, pltpu.roll(im_g, 64, 1)).astype(BF16)
            block_ref[block + 1] = jnp.where(lane < 64, pltpu.roll(re_g, 64, 1), im_g).astype(BF16)


def distance(group, k):
    turn = 2 * group + (k + 1) // 2
    return 8 - turn if k % 2 else 8 + turn


def one_hot(indices_ref, hot_ref, group, z, y):
    pick = iota((SLOTS, TILE), 1) == iota((SLOTS, TILE), 0) + SLOTS * y
    firsts, seconds = [], []
    for k in range(4):
        packed = indices_ref[(z + distance(group, k)) % NZ]
        first = row_of_station(lax.shift_right_logical(packed, 12), z).astype(F32)
        second = row_of_station(packed & 4095, z).astype(F32)
        firsts.append(jnp.sum(jnp.where(pick, first, 0.0), axis=1, keepdims=True))
        seconds.append(jnp.sum(jnp.where(pick, second, 0.0), axis=1, keepdims=True))
    rows = jnp.concatenate(firsts + seconds, axis=0).astype(I32)
    for far in range(2):
        column = iota((8 * SLOTS, HALF_ROWS), 1) + far * HALF_ROWS
        hot_ref[far, group] = jnp.where(column == rows, 1.0, 0.0).astype(BF16)


def cross_group(both, part_ref, group):
    straight, turned = 0.0, 0.0
    for s in range(NY):
        first = both[: 4 * SLOTS, 128 * s : 128 * (s + 1)]
        second = both[4 * SLOTS :, 128 * s : 128 * (s + 1)]
        straight = straight + first * second
        turned = turned + first * pltpu.roll(second, 64, 1)
    lane = iota((4 * SLOTS, 128), 1)
    value = jnp.where(lane < 64, straight + pltpu.roll(straight, 64, 1), turned - pltpu.roll(turned, 64, 1))
    for k in range(4):
        for core in range(NC):
            part_ref[core, 4 * group + k] = value[SLOTS * k + STA * core : SLOTS * k + STA * (core + 1)]


SEND_ORDER = (4, 12, 3, 13, 2, 14, 1, 15, 8, 7, 9, 6, 10, 5, 11)


def whole_kernel(
    count_in,
    wave_in,
    requests_in,
    pairs_in,
    forward_ref,
    out_ref,
    count_ref,
    wave_ref,
    requests_ref,
    pairs_ref,
    forward,
    block_ref,
    index_ref,
    all_ref,
    indices_ref,
    hot_ref,
    near_ref,
    part_ref,
    other_ref,
    stack_ref,
    final_ref,
    input_sem,
    table_sem,
    z_send,
    z_recv,
    i_send,
    i_recv,
    xy_send,
    xy_recv,
    c_send,
    c_recv,
    b_send,
    b_recv,
):
    z, x, y, c = where_am_i()
    z_peer = [at((z + d) % NZ, x, y, c) for d in range(NZ)]
    x_peer = [at(z, (x + d) % NX, y, c) for d in (2, 1, 3)]
    y_peer = [at(z, x, (y + d) % NY, c) for d in (2, 1, 3)]
    partner = at(z, x, y, 1 - c)
    peers = z_peer[1:] + x_peer + y_peer + [partner]

    inputs = [
        pltpu.make_async_copy(src, dst, input_sem.at[k])
        for k, (src, dst) in enumerate(
            ((wave_in, wave_ref), (requests_in, requests_ref), (pairs_in, pairs_ref), (count_in, count_ref))
        )
    ]
    tables = [pltpu.make_async_copy(forward_ref.at[r], forward.at[r], table_sem.at[r]) for r in range(4)]
    inputs[0].start()
    tables[0].start()
    tables[1].start()
    for copy in inputs[1:]:
        copy.start()
    signal_all(peers)
    inputs[0].wait()
    spec = []
    for r in range(4):
        tables[r].wait()
        if r < 2:
            tables[r + 2].start()
        spec.append(spectrum_part(wave_ref, forward.at[r], r))
    whiten(spec, block_ref)

    pl.semaphore_wait(pltpu.get_barrier_semaphore(), len(peers))

    def lanes(ys):
        return pl.ds(pl.multiple_of(ys * 128, 128), 128)

    def rows_of(d):
        away = (d + NEAR) % NZ
        return pl.ds(pl.multiple_of(away // 8 * HALF_ROWS + x * (8 * STA) + away % 8 * STA, STA), STA)

    def part(far, sub, xs, ys):
        rows = pl.ds(pl.multiple_of(far * HALF_ROWS + xs * (8 * STA) + sub * (4 * STA), 4 * STA), 4 * STA)
        return all_ref.at[rows, lanes(ys)]

    sent = []
    for d in SEND_ORDER:
        there = all_ref.at[rows_of(-d), lanes(y)]
        copy = remote(block_ref.at[(z + d) % NZ], there, z_send.at[d], z_recv.at[NZ - d], z_peer[d])
        copy.start()
        sent.append(copy)
    all_ref[rows_of(0), lanes(y)] = block_ref[z]

    def arrived(far, sub):
        for k in range(4):
            d = (8 * far + 4 * sub + k - NEAR) % NZ
            if d != 0:
                here = all_ref.at[rows_of(d), lanes(y)]
                remote(block_ref.at[0], here, z_send.at[0], z_recv.at[d], z_peer[1]).wait_recv()

    counter = [0]

    def give(far, sub, xs, ys, to):
        for peer in to:
            ref = part(far, sub, xs, ys)
            copy = remote(ref, ref, xy_send.at[counter[0]], xy_recv.at[2 * far + sub, xs, ys], peer)
            counter[0] += 1
            copy.start()
            sent.append(copy)

    def take(far, sub, xs, ys):
        ref = part(far, sub, xs, ys)
        remote(ref, ref, xy_send.at[0], xy_recv.at[2 * far + sub, xs, ys], z_peer[1]).wait_recv()

    def begin(far):
        arrived(far, 0)
        give(far, 0, x, y, x_peer)
        arrived(far, 1)
        give(far, 1, x, y, y_peer)
        give(far, 0, x, y, y_peer)
        give(far, 1, x, y, x_peer)

    def forward_on(far):
        for d in (3, 1, 2):
            xs, ys = (x + d) % NX, (y + d) % NY
            take(far, 0, xs, y)
            give(far, 0, xs, y, y_peer)
            take(far, 1, x, ys)
            give(far, 1, x, ys, x_peer)

    def settle(far):
        for d in (1, 3, 2):
            xs, ys = (x + d) % NX, (y + d) % NY
            take(far, 0, x, ys)
            take(far, 1, xs, y)
            for e in (1, 3, 2):
                take(far, 0, xs, (y + e) % NY)
                take(far, 1, (x + e) % NX, ys)

    for copy in inputs[1:]:
        copy.wait()
    index_ref[0] = pair_rows(count_ref, requests_ref, pairs_ref)
    begin(0)
    begin(1)
    for d in SEND_ORDER:
        copy = remote(index_ref.at[0], indices_ref.at[z], i_send.at[d], i_recv.at[NZ - d], z_peer[d])
        copy.start()
        sent.append(copy)
    indices_ref[z] = index_ref[0]
    forward_on(0)
    for d in range(1, NZ):
        zs = (z + d) % NZ
        remote(index_ref.at[0], indices_ref.at[zs], i_send.at[0], i_recv.at[d], z_peer[1]).wait_recv()
    forward_on(1)

    def hot_group(group, carry):
        one_hot(indices_ref, hot_ref, group, z, y)
        return carry

    lax.fori_loop(0, 4, hot_group, 0)
    settle(0)

    def near_group(group, carry):
        near_ref[group] = jnp.dot(hot_ref[0, group], all_ref[:HALF_ROWS], preferred_element_type=F32)
        return carry

    lax.fori_loop(0, 4, near_group, 0)
    settle(1)

    def swap(group):
        return remote(
            part_ref.at[1 - c, pl.ds(4 * group, 4)],
            other_ref.at[pl.ds(4 * group, 4)],
            c_send.at[group],
            c_recv.at[group],
            partner,
        )

    def back(group, k):
        d = distance(group, k)
        to = at((z + d) % NZ, x, y, c)
        return remote(stack_ref.at[4 * group + k], final_ref.at[z], b_send.at[4 * group + k], b_recv.at[(NZ - d) % NZ], to)

    def finish(group):
        swap(group).wait_recv()
        for k in range(4):
            place = 4 * group + k
            stack_ref[place] = (part_ref[c, place] + other_ref[place]).astype(BF16)
            if k < 3:
                back(group, k).start()
            else:

                @pl.when(group < 3)
                def _():
                    back(group, k).start()

    def group_step(group, carry):
        far = jnp.dot(hot_ref[1, group], all_ref[HALF_ROWS:], preferred_element_type=F32)
        cross_group(near_ref[group] + far, part_ref, group)
        swap(group).start()

        @pl.when(group > 0)
        def _():
            finish(group - 1)

        return carry

    lax.fori_loop(0, 4, group_step, 0)
    finish(3)
    final_ref[z] = stack_ref[NZ - 1]
    for d in range(1, NZ):
        here = final_ref.at[(z + d) % NZ]
        remote(stack_ref.at[0], here, b_send.at[0], b_recv.at[d], z_peer[1]).wait_recv()
    out_ref[...] = final_ref[...]
    for copy in sent:
        copy.wait_send()
    for group in range(4):
        swap(group).wait_send()
    for place in range(NZ - 1):
        back(place // 4, place % 4).wait_send()


def whole(count, wave, requests, pairs, forward):
    dma = pltpu.SemaphoreType.DMA
    vmem = pl.BlockSpec(memory_space=pltpu.VMEM)
    return pl.pallas_call(
        whole_kernel,
        out_shape=jax.ShapeDtypeStruct((NZ, STA, 128), BF16),
        in_specs=[pl.BlockSpec(memory_space=pltpu.HBM)] * 5,
        out_specs=vmem,
        scratch_shapes=[
            pltpu.SMEM((1,), I32),
            pltpu.VMEM(wave.shape, BF16),
            pltpu.VMEM(requests.shape, I32),
            pltpu.VMEM(pairs.shape, I32),
            pltpu.VMEM(forward.shape, BF16),
            pltpu.VMEM((NZ, STA, 128), BF16),
            pltpu.VMEM((1, 1, TILE), I32),
            pltpu.VMEM((ROWS, NY * 128), BF16),
            pltpu.VMEM((NZ, 1, TILE), I32),
            pltpu.VMEM((2, 4, 8 * SLOTS, HALF_ROWS), BF16),
            pltpu.VMEM((4, 8 * SLOTS, NY * 128), F32),
            pltpu.VMEM((NC, NZ, STA, 128), F32),
            pltpu.VMEM((NZ, STA, 128), F32),
            pltpu.VMEM((NZ, STA, 128), BF16),
            pltpu.VMEM((NZ, STA, 128), BF16),
            dma((4,)),
            dma((4,)),
            dma((NZ,)),
            dma((NZ,)),
            dma((NZ,)),
            dma((NZ,)),
            dma((4 * (NX * NY - 1),)),
            dma((4, NX, NY)),
            dma((4,)),
            dma((4,)),
            dma((NZ,)),
            dma((NZ,)),
        ],
        compiler_params=pltpu.CompilerParams(collective_id=0, has_side_effects=True, vmem_limit_bytes=VMEM_BYTES),
        name="whole",
    )(count, wave, requests, pairs, forward)


def lags_kernel(stack_ref, table_ref, out_ref):
    stack = [stack_ref[k] for k in range(NZ)]
    for chunk in range(QUARTER // CHUNK):
        lag_chunk(stack, table_ref.at[chunk], out_ref, chunk)


def lags(stacked, table):
    vmem = pl.BlockSpec(memory_space=pltpu.VMEM)
    return pl.pallas_call(
        lags_kernel,
        out_shape=jax.ShapeDtypeStruct((STA, LAGS), F32),
        in_specs=[vmem, vmem],
        out_specs=vmem,
        compiler_params=pltpu.CompilerParams(vmem_limit_bytes=LAGS_VMEM_BYTES),
        name="lags",
    )(stacked, table)


def lag_chunk(stack, table, out_ref, chunk):
    lane = iota((STA, 128), 1)
    sides = []
    for r in range(4):
        re, im = [], []
        for g in range(2):
            one = stack[4 * r + 2 * g].astype(F32)
            two = stack[4 * r + 2 * g + 1].astype(F32)
            re.append(jnp.where(lane < 64, one, pltpu.roll(two, 64, 1)))
            im.append(jnp.where(lane < 64, pltpu.roll(one, 64, 1), two))
        sides.append((jnp.concatenate(re, axis=1).astype(BF16), jnp.concatenate(im, axis=1).astype(BF16)))

    def dot(lhs, r, sine):
        rows = slice(SUB * r, SUB * (r + 1))
        return jnp.dot(lhs, table[rows, CHUNK * sine : CHUNK * (sine + 1)], preferred_element_type=F32)

    even, odd = [], []
    for r in (0, 2):
        even.append(dot(sides[r][0], r, 0) - dot(sides[r][1], r, 1))
    for r in (1, 3):
        lhs = jnp.concatenate(sides[r], axis=0)
        cos, sin = dot(lhs, r, 0), dot(lhs, r, 1)
        odd.append((cos[:STA] - sin[STA:], sin[:STA] + cos[STA:]))
    plus, minus = even[0] + even[1], even[0] - even[1]
    real = odd[0][0] + odd[1][0]
    imag = odd[0][1] - odd[1][1]

    def put(turns, value):
        lag = MAXLAG + QUARTER * turns + CHUNK * chunk
        if 0 <= lag < LAGS:
            out_ref[:, lag : lag + CHUNK] = value * (1.0 / math.sqrt(FB * NY * NC))

    put(0, plus + real)
    put(-2, plus - real)
    put(1, minus - imag)
    put(-1, minus + imag)


def body(forward, lag, waveform, requests, pair_list, pair_count):
    wave = waveform.reshape(STA, SAMPLES)
    pairs = jnp.swapaxes(pair_list, 1, 2).reshape(2, TILE)
    return lags(whole(pair_count, wave, requests, pairs, forward), lag)


def solution(mesh):
    forward, lag = wave_tables()
    in_specs = (P("pairs", "seg", None), P(), P("pairs", None, None), P("pairs"))
    out_specs = P(("pairs", "seg"), None)
    return jax.shard_map(
        functools.partial(body, forward, lag), mesh=mesh, in_specs=in_specs, out_specs=out_specs, check_vma=False
    )
```

```python
import functools
import math

import jax
import jax.numpy as jnp
import ml_dtypes
import numpy as np
from jax import lax
from jax.experimental import pallas as pl
from jax.experimental.pallas import tpu as pltpu
from jax.sharding import PartitionSpec as P

SAMPLES = 7680
K0 = 16
FB = 1024
HALF_WIN = 64
MAXLAG = 2560
LAGS = 5120
QUARTER = SAMPLES // 4
SUB = FB // 4
NZ, NX, NY, NC = 16, 4, 4, 2
STA = 32
TILE = 256
CHUNK = 640
DEAD = 4095
SLOTS = NC * STA
ROWS = NX * NZ * STA
HALF_ROWS = ROWS // 2
NEAR = 4
VMEM_BYTES = 56 * 1024 * 1024
F32 = jnp.float32
BF16 = jnp.bfloat16
I32 = jnp.int32


def wave_tables():
    bins = np.concatenate([K0 + 4 * np.arange(SUB) + r for r in range(4)])
    phase = (np.arange(QUARTER)[:, None] * bins[None, :]) % SAMPLES
    angle = phase.astype(np.float32) * np.float32(2.0 * math.pi / SAMPLES)
    cos = np.cos(angle).astype(ml_dtypes.bfloat16)
    sin = np.sin(angle).astype(ml_dtypes.bfloat16)
    forward = np.stack([np.concatenate([cos[:, SUB * r : SUB * (r + 1)], sin[:, SUB * r : SUB * (r + 1)]], axis=1) for r in range(4)])
    lag = np.stack(
        [
            np.concatenate([cos[CHUNK * i : CHUNK * (i + 1)].T, sin[CHUNK * i : CHUNK * (i + 1)].T], axis=1)
            for i in range(QUARTER // CHUNK)
        ]
    )
    return forward, lag


def iota(shape, dim):
    return lax.broadcasted_iota(I32, shape, dim)


def where_am_i():
    tile = lax.axis_index("pairs")
    seg = lax.axis_index("seg")
    return tile // NX, tile % NX, seg // NC, seg % NC


def at(z, x, y, c):
    return (z * NX + x, y * NC + c)


def row_of_station(station, z):
    owner = lax.shift_right_logical(station, 5)
    away = (lax.shift_right_logical(owner, 2) - z + NEAR) & (NZ - 1)
    row = lax.shift_right_logical(away, 3) * HALF_ROWS + (owner & 3) * (8 * STA) + (away & 7) * STA + (station & 31)
    return jnp.where(station == DEAD, -1, row)


def signal_all(peers):
    barrier = pltpu.get_barrier_semaphore()
    for peer in peers:
        pl.semaphore_signal(barrier, inc=1, device_id=peer, device_id_type=pl.DeviceIdType.MESH)


def remote(src, dst, send, recv, peer):
    return pltpu.make_async_remote_copy(
        src_ref=src, dst_ref=dst, send_sem=send, recv_sem=recv, device_id=peer, device_id_type=pl.DeviceIdType.MESH
    )


def pair_rows(count_ref, requests_ref, pairs_ref):
    tile = lax.axis_index("pairs")
    wanted = requests_ref[pl.ds(tile, 1), :].astype(F32)
    eye = iota((TILE, TILE), 0) == iota((TILE, TILE), 1)
    wanted_col = jnp.sum(jnp.where(eye, wanted, 0.0), axis=1, keepdims=True)
    ends = []
    for end in range(2):
        hit = iota((TILE, TILE), 0) == pairs_ref[end : end + 1, :]
        station = jnp.sum(jnp.where(hit, wanted_col, 0.0), axis=0, keepdims=True).astype(I32)
        ends.append(station)
    live = iota((1, TILE), 1) < count_ref[0]
    return jnp.where(live, ends[0] * 4096 + ends[1], DEAD * 4096 + DEAD)


def spectrum_part(wave_ref, table, r):
    def quarter(i):
        return wave_ref[:, QUARTER * i : QUARTER * (i + 1)].astype(F32)

    def times_table(lhs):
        return jnp.dot(lhs.astype(BF16), table[...], preferred_element_type=F32)

    if r % 2 == 0:
        sign = 1.0 - r
        out = times_table((quarter(0) + quarter(2)) + sign * (quarter(1) + quarter(3)))
        return out[:, :SUB], -out[:, SUB:]
    sign = r - 2.0
    out = times_table(jnp.concatenate([quarter(0) - quarter(2), quarter(1) - quarter(3)], axis=0))
    a_cos, a_sin = out[:STA, :SUB], out[:STA, SUB:]
    b_cos, b_sin = out[STA:, :SUB], out[STA:, SUB:]
    return a_cos + sign * b_sin, sign * b_cos - a_sin


def whiten(spec, block_ref):
    power = jnp.concatenate([re * re + im * im for re, im in spec], axis=0)
    high = power.astype(BF16)
    low = (power - high.astype(F32)).astype(BF16)
    parts = jnp.concatenate([high, low], axis=0)
    apart = iota((SUB, SUB), 0) - iota((SUB, SUB), 1)

    def band(lowest, highest):
        near = jnp.where((apart >= lowest) & (apart <= highest), 1.0, 0.0).astype(BF16)
        both = jnp.dot(parts, near, preferred_element_type=F32)
        return both[: 4 * STA] + both[4 * STA :]

    same = band(-16, 16)
    after = band(-15, 16)
    before = band(-16, 15)
    lane = iota((STA, 128), 1)
    for r in range(4):
        total = same[STA * r : STA * (r + 1)]
        for other in range(4):
            if other < r:
                total = total + after[STA * other : STA * (other + 1)]
            elif other > r:
                total = total + before[STA * other : STA * (other + 1)]
        j = 4 * iota((STA, SUB), 1) + r
        count = jnp.minimum(j + HALF_WIN, FB - 1) - jnp.maximum(j - HALF_WIN, 0) + 1
        scale = lax.rsqrt(total / count.astype(F32) + 1e-6)
        re = spec[r][0] * scale
        im = spec[r][1] * scale
        for g in range(2):
            re_g, im_g = re[:, 128 * g : 128 * (g + 1)], im[:, 128 * g : 128 * (g + 1)]
            block = 4 * r + 2 * g
            block_ref[block] = jnp.where(lane < 64, re_g, pltpu.roll(im_g, 64, 1)).astype(BF16)
            block_ref[block + 1] = jnp.where(lane < 64, pltpu.roll(re_g, 64, 1), im_g).astype(BF16)


def distance(group, k):
    turn = 2 * group + (k + 1) // 2
    return 8 - turn if k % 2 else 8 + turn


def one_hot(indices_ref, hot_ref, group, z, y):
    pick = iota((SLOTS, TILE), 1) == iota((SLOTS, TILE), 0) + SLOTS * y
    firsts, seconds = [], []
    for k in range(4):
        packed = indices_ref[(z + distance(group, k)) % NZ]
        first = row_of_station(lax.shift_right_logical(packed, 12), z).astype(F32)
        second = row_of_station(packed & 4095, z).astype(F32)
        firsts.append(jnp.sum(jnp.where(pick, first, 0.0), axis=1, keepdims=True))
        seconds.append(jnp.sum(jnp.where(pick, second, 0.0), axis=1, keepdims=True))
    rows = jnp.concatenate(firsts + seconds, axis=0).astype(I32)
    for far in range(2):
        column = iota((8 * SLOTS, HALF_ROWS), 1) + far * HALF_ROWS
        hot_ref[far, group] = jnp.where(column == rows, 1.0, 0.0).astype(BF16)


def cross_group(both, part_ref, group):
    straight, turned = 0.0, 0.0
    for s in range(NY):
        first = both[: 4 * SLOTS, 128 * s : 128 * (s + 1)]
        second = both[4 * SLOTS :, 128 * s : 128 * (s + 1)]
        straight = straight + first * second
        turned = turned + first * pltpu.roll(second, 64, 1)
    lane = iota((4 * SLOTS, 128), 1)
    value = jnp.where(lane < 64, straight + pltpu.roll(straight, 64, 1), turned - pltpu.roll(turned, 64, 1))
    for k in range(4):
        for core in range(NC):
            part_ref[core, 4 * group + k] = value[SLOTS * k + STA * core : SLOTS * k + STA * (core + 1)]


SEND_ORDER = (4, 12, 3, 13, 2, 14, 1, 15, 8, 7, 9, 6, 10, 5, 11)


def whole_kernel(
    count_in,
    wave_in,
    requests_in,
    pairs_in,
    forward_ref,
    lag_ref,
    out_ref,
    count_ref,
    wave_ref,
    requests_ref,
    pairs_ref,
    forward,
    lag,
    block_ref,
    index_ref,
    all_ref,
    indices_ref,
    hot_ref,
    near_ref,
    part_ref,
    other_ref,
    stack_ref,
    final_ref,
    input_sem,
    table_sem,
    z_send,
    z_recv,
    i_send,
    i_recv,
    xy_send,
    xy_recv,
    c_send,
    c_recv,
    b_send,
    b_recv,
):
    z, x, y, c = where_am_i()
    z_peer = [at((z + d) % NZ, x, y, c) for d in range(NZ)]
    x_peer = [at(z, (x + d) % NX, y, c) for d in (2, 1, 3)]
    y_peer = [at(z, x, (y + d) % NY, c) for d in (2, 1, 3)]
    partner = at(z, x, y, 1 - c)
    peers = z_peer[1:] + x_peer + y_peer + [partner]

    inputs = [
        pltpu.make_async_copy(src, dst, input_sem.at[k])
        for k, (src, dst) in enumerate(
            ((wave_in, wave_ref), (requests_in, requests_ref), (pairs_in, pairs_ref), (count_in, count_ref))
        )
    ]
    tables = [pltpu.make_async_copy(forward_ref.at[r], forward.at[r], table_sem.at[r]) for r in range(4)]
    tables.append(pltpu.make_async_copy(lag_ref, lag, table_sem.at[4]))
    inputs[0].start()
    tables[0].start()
    tables[1].start()
    for copy in inputs[1:]:
        copy.start()
    signal_all(peers)
    inputs[0].wait()
    spec = []
    for r in range(4):
        tables[r].wait()
        if r < 2:
            tables[r + 2].start()
        spec.append(spectrum_part(wave_ref, forward.at[r], r))
    whiten(spec, block_ref)

    pl.semaphore_wait(pltpu.get_barrier_semaphore(), len(peers))

    def lanes(ys):
        return pl.ds(pl.multiple_of(ys * 128, 128), 128)

    def rows_of(d):
        away = (d + NEAR) % NZ
        return pl.ds(pl.multiple_of(away // 8 * HALF_ROWS + x * (8 * STA) + away % 8 * STA, STA), STA)

    def part(far, sub, xs, ys):
        rows = pl.ds(pl.multiple_of(far * HALF_ROWS + xs * (8 * STA) + sub * (4 * STA), 4 * STA), 4 * STA)
        return all_ref.at[rows, lanes(ys)]

    sent = []
    for d in SEND_ORDER:
        there = all_ref.at[rows_of(-d), lanes(y)]
        copy = remote(block_ref.at[(z + d) % NZ], there, z_send.at[d], z_recv.at[NZ - d], z_peer[d])
        copy.start()
        sent.append(copy)
    all_ref[rows_of(0), lanes(y)] = block_ref[z]

    def arrived(far, sub):
        for k in range(4):
            d = (8 * far + 4 * sub + k - NEAR) % NZ
            if d != 0:
                here = all_ref.at[rows_of(d), lanes(y)]
                remote(block_ref.at[0], here, z_send.at[0], z_recv.at[d], z_peer[1]).wait_recv()

    counter = [0]

    def give(far, sub, xs, ys, to):
        for peer in to:
            ref = part(far, sub, xs, ys)
            copy = remote(ref, ref, xy_send.at[counter[0]], xy_recv.at[2 * far + sub, xs, ys], peer)
            counter[0] += 1
            copy.start()
            sent.append(copy)

    def take(far, sub, xs, ys):
        ref = part(far, sub, xs, ys)
        remote(ref, ref, xy_send.at[0], xy_recv.at[2 * far + sub, xs, ys], z_peer[1]).wait_recv()

    def begin(far):
        arrived(far, 0)
        give(far, 0, x, y, x_peer)
        arrived(far, 1)
        give(far, 1, x, y, y_peer)

    def own_on(far):
        give(far, 0, x, y, y_peer)
        give(far, 1, x, y, x_peer)

    def forward_on(far):
        for d in (3, 1, 2):
            xs, ys = (x + d) % NX, (y + d) % NY
            take(far, 0, xs, y)
            give(far, 0, xs, y, y_peer)
            take(far, 1, x, ys)
            give(far, 1, x, ys, x_peer)

    def settle(far):
        for d in (1, 3, 2):
            xs, ys = (x + d) % NX, (y + d) % NY
            take(far, 0, x, ys)
            take(far, 1, xs, y)
            for e in (1, 3, 2):
                take(far, 0, xs, (y + e) % NY)
                take(far, 1, (x + e) % NX, ys)

    for copy in inputs[1:]:
        copy.wait()
    index_ref[0] = pair_rows(count_ref, requests_ref, pairs_ref)
    begin(0)
    own_on(0)
    begin(1)
    for d in SEND_ORDER:
        copy = remote(index_ref.at[0], indices_ref.at[z], i_send.at[d], i_recv.at[NZ - d], z_peer[d])
        copy.start()
        sent.append(copy)
    indices_ref[z] = index_ref[0]
    forward_on(0)
    own_on(1)
    for d in range(1, NZ):
        zs = (z + d) % NZ
        remote(index_ref.at[0], indices_ref.at[zs], i_send.at[0], i_recv.at[d], z_peer[1]).wait_recv()
    forward_on(1)

    def hot_group(group, carry):
        one_hot(indices_ref, hot_ref, group, z, y)
        return carry

    lax.fori_loop(0, 4, hot_group, 0)
    settle(0)

    def near_group(group, carry):
        near_ref[group] = jnp.dot(hot_ref[0, group], all_ref[:HALF_ROWS], preferred_element_type=F32)
        return carry

    tables[4].start()
    lax.fori_loop(0, 4, near_group, 0)
    settle(1)

    def swap(group):
        return remote(
            part_ref.at[1 - c, pl.ds(4 * group, 4)],
            other_ref.at[pl.ds(4 * group, 4)],
            c_send.at[group],
            c_recv.at[group],
            partner,
        )

    def back(group, k):
        d = distance(group, k)
        to = at((z + d) % NZ, x, y, c)
        return remote(stack_ref.at[4 * group + k], final_ref.at[z], b_send.at[4 * group + k], b_recv.at[(NZ - d) % NZ], to)

    def finish(group):
        swap(group).wait_recv()
        for k in range(4):
            place = 4 * group + k
            stack_ref[place] = (part_ref[c, place] + other_ref[place]).astype(BF16)
            if k < 3:
                back(group, k).start()
            else:

                @pl.when(group < 3)
                def _():
                    back(group, k).start()

    def group_step(group, carry):
        far = jnp.dot(hot_ref[1, group], all_ref[HALF_ROWS:], preferred_element_type=F32)
        cross_group(near_ref[group] + far, part_ref, group)
        swap(group).start()

        @pl.when(group > 0)
        def _():
            finish(group - 1)

        return carry

    lax.fori_loop(0, 4, group_step, 0)
    finish(3)
    final_ref[z] = stack_ref[NZ - 1]
    for d in range(1, NZ):
        here = final_ref.at[(z + d) % NZ]
        remote(stack_ref.at[0], here, b_send.at[0], b_recv.at[d], z_peer[1]).wait_recv()
    tables[4].wait()
    stack = [final_ref[k] for k in range(NZ)]
    for chunk in range(QUARTER // CHUNK):
        lag_chunk(stack, lag.at[chunk], out_ref, chunk)
    for copy in sent:
        copy.wait_send()
    for group in range(4):
        swap(group).wait_send()
    for place in range(NZ - 1):
        back(place // 4, place % 4).wait_send()


def whole(count, wave, requests, pairs, forward, lag):
    dma = pltpu.SemaphoreType.DMA
    vmem = pl.BlockSpec(memory_space=pltpu.VMEM)
    return pl.pallas_call(
        whole_kernel,
        out_shape=jax.ShapeDtypeStruct((STA, LAGS), F32),
        in_specs=[pl.BlockSpec(memory_space=pl.ANY)] * 6,
        out_specs=vmem,
        scratch_shapes=[
            pltpu.SMEM((1,), I32),
            pltpu.VMEM(wave.shape, BF16),
            pltpu.VMEM(requests.shape, I32),
            pltpu.VMEM(pairs.shape, I32),
            pltpu.VMEM(forward.shape, BF16),
            pltpu.VMEM(lag.shape, BF16),
            pltpu.VMEM((NZ, STA, 128), BF16),
            pltpu.VMEM((1, 1, TILE), I32),
            pltpu.VMEM((ROWS, NY * 128), BF16),
            pltpu.VMEM((NZ, 1, TILE), I32),
            pltpu.VMEM((2, 4, 8 * SLOTS, HALF_ROWS), BF16),
            pltpu.VMEM((4, 8 * SLOTS, NY * 128), F32),
            pltpu.VMEM((NC, NZ, STA, 128), F32),
            pltpu.VMEM((NZ, STA, 128), F32),
            pltpu.VMEM((NZ, STA, 128), BF16),
            pltpu.VMEM((NZ, STA, 128), BF16),
            dma((4,)),
            dma((5,)),
            dma((NZ,)),
            dma((NZ,)),
            dma((NZ,)),
            dma((NZ,)),
            dma((4 * (NX * NY - 1),)),
            dma((4, NX, NY)),
            dma((4,)),
            dma((4,)),
            dma((NZ,)),
            dma((NZ,)),
        ],
        compiler_params=pltpu.CompilerParams(collective_id=0, has_side_effects=True, vmem_limit_bytes=VMEM_BYTES),
        name="whole",
    )(count, wave, requests, pairs, forward, lag)


def lag_chunk(stack, table, out_ref, chunk):
    lane = iota((STA, 128), 1)
    sides = []
    for r in range(4):
        re, im = [], []
        for g in range(2):
            one = stack[4 * r + 2 * g].astype(F32)
            two = stack[4 * r + 2 * g + 1].astype(F32)
            re.append(jnp.where(lane < 64, one, pltpu.roll(two, 64, 1)))
            im.append(jnp.where(lane < 64, pltpu.roll(one, 64, 1), two))
        sides.append((jnp.concatenate(re, axis=1).astype(BF16), jnp.concatenate(im, axis=1).astype(BF16)))

    def dot(lhs, r, sine):
        rows = slice(SUB * r, SUB * (r + 1))
        return jnp.dot(lhs, table[rows, CHUNK * sine : CHUNK * (sine + 1)], preferred_element_type=F32)

    even, odd = [], []
    for r in (0, 2):
        even.append(dot(sides[r][0], r, 0) - dot(sides[r][1], r, 1))
    for r in (1, 3):
        lhs = jnp.concatenate(sides[r], axis=0)
        cos, sin = dot(lhs, r, 0), dot(lhs, r, 1)
        odd.append((cos[:STA] - sin[STA:], sin[:STA] + cos[STA:]))
    plus, minus = even[0] + even[1], even[0] - even[1]
    real = odd[0][0] + odd[1][0]
    imag = odd[0][1] - odd[1][1]

    def put(turns, value):
        lag = MAXLAG + QUARTER * turns + CHUNK * chunk
        if 0 <= lag < LAGS:
            out_ref[:, lag : lag + CHUNK] = value

    put(0, plus + real)
    put(-2, plus - real)
    put(1, minus - imag)
    put(-1, minus + imag)


def body(forward, lag, waveform, requests, pair_list, pair_count):
    wave = waveform.reshape(STA, SAMPLES)
    pairs = jnp.swapaxes(pair_list, 1, 2).reshape(2, TILE)
    return whole(pair_count, wave, requests, pairs, forward, lag) * (1.0 / math.sqrt(FB * NY * NC))


def solution(mesh):
    forward, lag = wave_tables()
    in_specs = (P("pairs", "seg", None), P(), P("pairs", None, None), P("pairs"))
    out_specs = P(("pairs", "seg"), None)
    return jax.shard_map(
        functools.partial(body, forward, lag), mesh=mesh, in_specs=in_specs, out_specs=out_specs, check_vma=False
    )
```
